32 devices in a mesh: band: 8 (over z, y), slab: 4 (over x, core).
Axes of the slice: x: 2, y: 2, z: 4, core: 2. Of those that a mesh axis runs over, the one named last changes fastest.
Arguments:
- bands: float32 [32, 32, 24, 128], P('band', 'slab'), may hold values from -8 to 8
- potential: float32 [32, 24, 128], P('slab'), may hold values from -1 to 0
Outputs:
- filtered: float32 [32, 32, 24, 128], P('band', 'slab')
- correlation: float32 [32, 32], P('band')
- projected: float32 [32, 32], P('band')
The draws below stay inside these ranges and needn't reach their ends.
All inputs are finite; a program needn't handle non-finite values.
Results may differ from the reference program's by a relative error of at most 0.000092.
Values sent between devices are 32-bit elements; how exact they have to be, the bound alone decides.
A program may use at most 128 MiB of HBM per device.

```python
import jax
import jax.numpy as jnp
from jax import lax

BANDS = 32
NY = 24
NX = 128
NZ = 32


def draw_bands(key, part):
    base = jax.random.fold_in(key, 11)
    first, second, third = jax.random.split(base, 3)
    common = jax.random.normal(second, (1, NZ, NY, NX), jnp.float32)
    mixing = jax.random.uniform(third, (BANDS, 1, 1, 1), jnp.float32, 0.3, 1.0)
    noise = jax.random.normal(first, (BANDS, NZ, NY, NX), jnp.float32)
    values = noise + mixing * common
    return jnp.clip(values, -8.0, 8.0)


def shard_levels(stream_key, shape, shards, least, largest):
    gain, own = 1.0, jax.random.fold_in(stream_key, 6)
    for position, parts in shards:
        steps = jnp.exp(jax.random.uniform(jax.random.fold_in(own, position), (parts,), jnp.float32, least / len(shards), largest / len(shards)))
        gain = gain * jnp.repeat(steps, shape[position] // parts).reshape([-1 if axis == position else 1 for axis in range(len(shape))])
    return gain


def setup_inputs(seed: int = 0) -> dict:
    streams_of = jax.random.split(jax.random.key(seed), 3)
    bands = draw_bands(jax.random.fold_in(streams_of[2], 71), 0)
    potential = jnp.clip(-1.0 + 1.0 * jax.random.uniform(streams_of[1], (NZ, NY, NX), jnp.float32) ** shard_levels(streams_of[1], (NZ, NY, NX), ((0, 4),), -0.2, 0.2), -1.0, 0.0)
    return {"bands": bands, "potential": potential}


centre = 4.5
half = 3.5


def hamiltonian(field, potential):
    lap = jnp.zeros_like(field)
    for axis in (1, 2, 3):
        lap = lap - 2.5 * field
        lap = lap + (4.0 / 3.0) * (jnp.roll(field, 1, axis) + jnp.roll(field, -1, axis))
        lap = lap - (1.0 / 12.0) * (jnp.roll(field, 2, axis) + jnp.roll(field, -2, axis))
    return -0.5 * lap + potential[None] * field


def reference(bands, potential):
    previous = bands
    current = (hamiltonian(bands, potential) - centre * bands) / half
    for step in range(3):
        following = 2.0 * (hamiltonian(current, potential) - centre * current) / half - previous
        previous, current = current, following
    image = hamiltonian(current, potential)
    volume = 1.0 / (NX * NY * NZ)
    flat = current.reshape(BANDS, -1)
    himage = image.reshape(BANDS, -1)
    correlation = jnp.dot(flat, flat.T, precision=lax.Precision.HIGHEST, preferred_element_type=jnp.float32) * volume
    projected = jnp.dot(himage, flat.T, precision=lax.Precision.HIGHEST, preferred_element_type=jnp.float32) * volume
    return current, correlation, projected
```

```python
import functools

import jax
import jax.numpy as jnp
from jax import lax
from jax.experimental import pallas as pl
from jax.experimental.pallas import tpu as pltpu
from jax.sharding import PartitionSpec as P

centre = 4.5
half = 3.5
MESH = pl.DeviceIdType.MESH
STEPS = 4


def shifted(v, axis):
    n = v.shape[axis]
    near = pltpu.roll(v, 1, axis) + pltpu.roll(v, n - 1, axis)
    far = pltpu.roll(v, 2, axis) + pltpu.roll(v, n - 2, axis)
    return near, far


def kernel(
    dims, bands, pot, f_out, c_out, p_out,
    e, vbuf, img, fall, iall, part, rb, rs,
    halo_send, halo_recv, load_sem, out_sem, gram_send, gram_recv,
    row_send, row_recv, slab_send, slab_recv,
):
    nb, ns, L, nz, ny, chunk, active, volume = dims
    b, s = lax.axis_index("band"), lax.axis_index("slab")
    up, down = lax.rem(s + 1, ns), lax.rem(s + ns - 1, ns)
    inner = pl.ds(2 * ny, nz * ny)

    load = pltpu.make_async_copy(bands, e.at[0, :, inner], load_sem.at[0])
    load.start()
    load_pot = pltpu.make_async_copy(pot, vbuf, load_sem.at[1])
    load_pot.start()

    barrier = pltpu.get_barrier_semaphore()

    def greet_band(d, carry):
        pl.semaphore_signal(
            barrier, inc=1, device_id={"band": lax.rem(b + d, nb)}, device_id_type=MESH
        )
        return carry

    lax.fori_loop(1, nb, greet_band, 0)
    for d in range(1, ns):
        pl.semaphore_signal(
            barrier, inc=1, device_id={"slab": lax.rem(s + d, ns)}, device_id_type=MESH
        )
    pl.semaphore_wait(barrier, nb - 1 + ns - 1)

    def halo(k):
        if k == 0:
            low, high = bands.at[:, pl.ds(0, 2 * ny)], bands.at[:, pl.ds((nz - 2) * ny, 2 * ny)]
        else:
            low, high = e.at[k, :, pl.ds(2 * ny, 2 * ny)], e.at[k, :, pl.ds(nz * ny, 2 * ny)]
        return (
            pltpu.make_async_remote_copy(
                src_ref=low,
                dst_ref=e.at[k, :, pl.ds((nz + 2) * ny, 2 * ny)],
                send_sem=halo_send.at[k, 0],
                recv_sem=halo_recv.at[k, 0],
                device_id={"slab": down},
                device_id_type=MESH,
            ),
            pltpu.make_async_remote_copy(
                src_ref=high,
                dst_ref=e.at[k, :, pl.ds(0, 2 * ny)],
                send_sem=halo_send.at[k, 1],
                recv_sem=halo_recv.at[k, 1],
                device_id={"slab": up},
                device_id_type=MESH,
            ),
        )

    def plane(k, z):
        def rows(offset):
            return pl.ds(pl.multiple_of((z + 2 + offset) * ny, 8), ny)

        here = pl.ds(pl.multiple_of(z * ny, 8), ny)
        scale = 1.0 if k == STEPS else (1.0 if k == 0 else 2.0) / half
        shift = 3.75 if k == STEPS else 3.75 - centre
        diagonal = (vbuf[here, :] + shift) * scale
        for l in range(L):
            v = e[k, l, rows(0), :]
            near = e[k, l, rows(-1), :] + e[k, l, rows(1), :]
            far = e[k, l, rows(-2), :] + e[k, l, rows(2), :]
            for axis in (0, 1):
                n1, n2 = shifted(v, axis)
                near = near + n1
                far = far + n2
            value = diagonal * v - (scale * 2.0 / 3.0) * near + (scale / 24.0) * far
            if k == STEPS:
                img[l, here, :] = value
            else:
                if k > 0:
                    value = value - e[k - 1, l, rows(0), :]
                e[k + 1, l, rows(0), :] = value

    def planes(k, start, stop):
        def step(z, carry):
            plane(k, z)
            return carry

        lax.fori_loop(start, stop, step, 0)

    def regroup(which, d, back=False):
        peer = lax.rem(b + d, nb)
        cells = pl.multiple_of(peer * chunk, 8)
        if which == 0:
            src = e.at[STEPS, :, pl.ds(2 * ny + cells, chunk)]
        else:
            src = img.at[:, pl.ds(cells, chunk)]
        return pltpu.make_async_remote_copy(
            src_ref=src,
            dst_ref=(fall, iall)[which].at[b],
            send_sem=gram_send.at[which, d],
            recv_sem=gram_recv.at[which, d],
            device_id={"band": peer},
            device_id_type=MESH,
        ), peer

    def regroup_start(which):
        def step(d, carry):
            copy, peer = regroup(which, d)
            if active == nb:
                copy.start()
            else:
                @pl.when(peer < active)
                def _():
                    copy.start()
            return carry

        lax.fori_loop(1, nb, step, 0)

    def regroup_own(which):
        mine = pl.multiple_of(b * chunk, 8)
        if which == 0:
            fall[b] = e[STEPS, :, pl.ds(2 * ny + mine, chunk), :]
        else:
            iall[b] = img[:, pl.ds(mine, chunk), :]

    def regroup_arrive(which):
        def step(d, carry):
            copy, _ = regroup(which, d)
            copy.wait_recv()
            return carry

        lax.fori_loop(1, nb, step, 0)

    def regroup_sent(which):
        def step(d, carry):
            copy, peer = regroup(which, d)
            if active == nb:
                copy.wait_send()
            else:
                @pl.when(peer < active)
                def _():
                    copy.wait_send()
            return carry

        lax.fori_loop(1, nb, step, 0)

    def cells_of(ref):
        flat = ref.reshape(nb * L * chunk, ref.shape[-1])
        return jnp.concatenate(
            [flat[pl.ds(r, nb * L, stride=chunk), :] for r in range(chunk)], axis=1
        )

    def product(x, y):
        return lax.dot_general(
            x, y, (((1,), (1,)), ((), ())),
            precision=lax.Precision.HIGHEST, preferred_element_type=jnp.float32,
        )

    def working(action):
        if active == nb:
            action()
        else:
            pl.when(b < active)(action)

    for copy in halo(0):
        copy.start()
    load.wait()
    load_pot.wait()
    for k in range(STEPS):
        if k == 0:
            planes(0, 2, nz - 2)
        for copy in halo(k):
            copy.wait_recv()
        planes(k, 0, 2)
        planes(k, nz - 2, nz)
        for copy in halo(k + 1):
            copy.start()
        if k > 0:
            planes(k, 2, nz - 2)
    regroup_start(0)
    result = pltpu.make_async_copy(e.at[STEPS, :, inner], f_out, out_sem)
    result.start()
    planes(STEPS, 2, nz - 2)
    for copy in halo(STEPS):
        copy.wait_recv()
    planes(STEPS, 0, 2)
    planes(STEPS, nz - 2, nz)
    regroup_start(1)

    def correlate():
        regroup_own(0)
        regroup_own(1)
        regroup_arrive(0)
        fs = cells_of(fall)
        gram = product(fs, fs) * volume
        for g in range(nb):
            part[g, 0:L, :] = gram[g * L:(g + 1) * L]
        regroup_arrive(1)
        proj = product(cells_of(iall), cells_of(fall)) * volume
        for g in range(nb):
            part[g, L:2 * L, :] = proj[g * L:(g + 1) * L]

    working(correlate)
    if active != nb:
        @pl.when(b >= active)
        def _():
            part[...] = jnp.zeros_like(part)

    def row(d):
        peer = lax.rem(b + d, nb)
        return pltpu.make_async_remote_copy(
            src_ref=part.at[peer],
            dst_ref=rb.at[b],
            send_sem=row_send.at[d],
            recv_sem=row_recv.at[d],
            device_id={"band": peer},
            device_id_type=MESH,
        )

    def each_row(action):
        def step(d, carry):
            action(row(d))
            return carry

        lax.fori_loop(1, nb, step, 0)

    each_row(lambda copy: copy.start())
    rb[b] = part[b]
    each_row(lambda copy: copy.wait_recv())
    rs[s] = jnp.sum(rb[...], axis=0)

    def across(d):
        return pltpu.make_async_remote_copy(
            src_ref=rs.at[s],
            dst_ref=rs.at[s],
            send_sem=slab_send.at[d],
            recv_sem=slab_recv.at[d],
            device_id={"slab": lax.rem(s + d, ns)},
            device_id_type=MESH,
        )

    for d in range(1, ns):
        across(d).start()
    for d in range(1, ns):
        across(d).wait_recv()
    total = rs[0]
    for other in range(1, ns):
        total = total + rs[other]
    c_out[...] = total[:L]
    p_out[...] = total[L:]
    for d in range(1, ns):
        across(d).wait_send()
    each_row(lambda copy: copy.wait_send())
    for k in range(STEPS + 1):
        for copy in halo(k):
            copy.wait_send()
    regroup_sent(0)
    regroup_sent(1)
    result.wait()


def body(bands, potential):
    L, nz, ny, nx = bands.shape
    nb, ns = lax.axis_size("band"), lax.axis_size("slab")
    rows = nz * ny
    tiles = rows // 8
    each = -(-tiles // nb)
    while tiles % each:
        each += 1
    chunk = each * 8
    active = rows // chunk
    dims = (nb, ns, L, nz, ny, chunk, active, 1.0 / (rows * ns * nx))
    f32 = jnp.float32
    anywhere, vmem = pl.BlockSpec(memory_space=pl.ANY), pl.BlockSpec(memory_space=pltpu.VMEM)
    dma = pltpu.SemaphoreType.DMA
    f, c, p = pl.pallas_call(
        functools.partial(kernel, dims),
        out_shape=(
            jax.ShapeDtypeStruct((L, rows, nx), f32),
            jax.ShapeDtypeStruct((L, nb * L), f32),
            jax.ShapeDtypeStruct((L, nb * L), f32),
        ),
        in_specs=[anywhere, anywhere],
        out_specs=(anywhere, vmem, vmem),
        scratch_shapes=[
            pltpu.VMEM((STEPS + 1, L, (nz + 4) * ny, nx), f32),
            pltpu.VMEM((rows, nx), f32),
            pltpu.VMEM((L, rows, nx), f32),
            pltpu.VMEM((nb, L, chunk, nx), f32),
            pltpu.VMEM((nb, L, chunk, nx), f32),
            pltpu.VMEM((nb, 2 * L, nb * L), f32),
            pltpu.VMEM((nb, 2 * L, nb * L), f32),
            pltpu.VMEM((ns, 2 * L, nb * L), f32),
            dma((STEPS + 1, 2)), dma((STEPS + 1, 2)),
            dma((2,)), dma,
            dma((2, nb)), dma((2, nb)),
            dma((nb,)), dma((nb,)),
            dma((ns,)), dma((ns,)),
        ],
        compiler_params=pltpu.CompilerParams(
            collective_id=0, has_side_effects=True, vmem_limit_bytes=40 * 1024 * 1024
        ),
    )(bands.reshape(L, rows, nx), potential.reshape(rows, nx))
    return f.reshape(L, nz, ny, nx), c, p


def solution(mesh):
    in_specs = (P("band", "slab", None, None), P("slab", None, None))
    out_specs = (P("band", "slab", None, None), P("band", None), P("band", None))
    return jax.shard_map(body, mesh=mesh, in_specs=in_specs, out_specs=out_specs, check_vma=False)
```

```python
import functools

import jax
import jax.numpy as jnp
from jax import lax
from jax.experimental import pallas as pl
from jax.experimental.pallas import tpu as pltpu
from jax.sharding import PartitionSpec as P

centre = 4.5
half = 3.5
MESH = pl.DeviceIdType.MESH
STEPS = 4


def shifted(v, axis):
    n = v.shape[axis]
    near = pltpu.roll(v, 1, axis) + pltpu.roll(v, n - 1, axis)
    far = pltpu.roll(v, 2, axis) + pltpu.roll(v, n - 2, axis)
    return near, far


def kernel(
    dims, bands, pot, f_out, cp_out,
    e, vbuf, img, fall, iall, fhi, flo, part, rb, rs,
    halo_send, halo_recv, load_sem, out_sem, gram_send, gram_recv,
    row_send, row_recv, slab_send, slab_recv,
):
    nb, ns, L, nz, ny, chunk, active, volume = dims
    b, s = lax.axis_index("band"), lax.axis_index("slab")
    up, down = lax.rem(s + 1, ns), lax.rem(s + ns - 1, ns)
    inner = pl.ds(2 * ny, nz * ny)

    load = pltpu.make_async_copy(bands, e.at[0, :, inner], load_sem.at[0])
    load.start()
    load_pot = pltpu.make_async_copy(pot, vbuf, load_sem.at[1])
    load_pot.start()

    barrier = pltpu.get_barrier_semaphore()

    def greet_band(d, carry):
        pl.semaphore_signal(
            barrier, inc=1, device_id={"band": lax.rem(b + d, nb)}, device_id_type=MESH
        )
        return carry

    lax.fori_loop(1, nb, greet_band, 0)
    for d in range(1, ns):
        pl.semaphore_signal(
            barrier, inc=1, device_id={"slab": lax.rem(s + d, ns)}, device_id_type=MESH
        )
    pl.semaphore_wait(barrier, nb - 1 + ns - 1)

    def halo(k, l):
        if k == 0:
            low, high = bands.at[l, pl.ds(0, 2 * ny)], bands.at[l, pl.ds((nz - 2) * ny, 2 * ny)]
        else:
            low, high = e.at[k, l, pl.ds(2 * ny, 2 * ny)], e.at[k, l, pl.ds(nz * ny, 2 * ny)]
        return (
            pltpu.make_async_remote_copy(
                src_ref=low,
                dst_ref=e.at[k, l, pl.ds((nz + 2) * ny, 2 * ny)],
                send_sem=halo_send.at[k, l, 0],
                recv_sem=halo_recv.at[k, l, 0],
                device_id={"slab": down},
                device_id_type=MESH,
            ),
            pltpu.make_async_remote_copy(
                src_ref=high,
                dst_ref=e.at[k, l, pl.ds(0, 2 * ny)],
                send_sem=halo_send.at[k, l, 1],
                recv_sem=halo_recv.at[k, l, 1],
                device_id={"slab": up},
                device_id_type=MESH,
            ),
        )

    def plane(k, l, z):
        def rows(offset):
            start = (z + 2 + offset) * ny
            return pl.ds(start if isinstance(z, int) else pl.multiple_of(start, 8), ny)

        here = pl.ds(z * ny if isinstance(z, int) else pl.multiple_of(z * ny, 8), ny)
        scale = 1.0 if k == STEPS else (1.0 if k == 0 else 2.0) / half
        shift = 3.75 if k == STEPS else 3.75 - centre
        diagonal = (vbuf[here, :] + shift) * scale
        v = e[k, l, rows(0), :]
        near = e[k, l, rows(-1), :] + e[k, l, rows(1), :]
        far = e[k, l, rows(-2), :] + e[k, l, rows(2), :]
        for axis in (0, 1):
            n1, n2 = shifted(v, axis)
            near = near + n1
            far = far + n2
        value = diagonal * v - (scale * 2.0 / 3.0) * near + (scale / 24.0) * far
        if k == STEPS:
            img[l, here, :] = value
        else:
            if k > 0:
                value = value - e[k - 1, l, rows(0), :]
            e[k + 1, l, rows(0), :] = value

    def inside(k, l):
        for z in range(2, nz - 2):
            plane(k, l, z)

    def edges(k, l):
        for copy in halo(k, l):
            copy.wait_recv()
        for z in (0, 1, nz - 2, nz - 1):
            plane(k, l, z)

    def regroup(which, d, l):
        peer = lax.rem(b + d, nb)
        cells = pl.multiple_of(peer * chunk, 8)
        if which == 0:
            src = e.at[STEPS, l, pl.ds(2 * ny + cells, chunk)]
        else:
            src = img.at[l, pl.ds(cells, chunk)]
        return pltpu.make_async_remote_copy(
            src_ref=src,
            dst_ref=(fall, iall)[which].at[b, l],
            send_sem=gram_send.at[which, d, l],
            recv_sem=gram_recv.at[which, d, l],
            device_id={"band": peer},
            device_id_type=MESH,
        ), peer

    def when_active(peer, action):
        if active == nb:
            action()
        else:
            pl.when(peer < active)(action)

    def regroup_start(which, l):
        def step(d, carry):
            copy, peer = regroup(which, d, l)
            when_active(peer, copy.start)
            return carry

        lax.fori_loop(1, nb, step, 0)

    def regroup_sent(which):
        def step(d, carry):
            for l in range(L):
                copy, peer = regroup(which, d, l)
                when_active(peer, copy.wait_send)
            return carry

        lax.fori_loop(1, nb, step, 0)

    def regroup_own(which):
        mine = pl.multiple_of(b * chunk, 8)
        if which == 0:
            fall[b] = e[STEPS, :, pl.ds(2 * ny + mine, chunk), :]
        else:
            iall[b] = img[:, pl.ds(mine, chunk), :]

    def regroup_arrive(which):
        def step(d, carry):
            for l in range(L):
                regroup(which, d, l)[0].wait_recv()
            return carry

        lax.fori_loop(1, nb, step, 0)

    def halves_of(ref):
        flat = ref.reshape(nb * L * chunk, ref.shape[-1])
        whole = jnp.concatenate(
            [flat[pl.ds(r, nb * L, stride=chunk), :] for r in range(chunk)], axis=1
        )
        high = whole.astype(jnp.bfloat16)
        return high, (whole - high.astype(jnp.float32)).astype(jnp.bfloat16)

    def product(high, low):
        both = jnp.concatenate([high, low], axis=0)
        out = sum(
            lax.dot_general(
                both, other[...], (((1,), (1,)), ((), ())),
                preferred_element_type=jnp.float32,
            )
            for other in (flo, fhi)
        )
        return (out[nb * L:] + out[:nb * L]) * volume

    for l in range(L):
        for copy in halo(0, l):
            copy.start()
    load.wait()
    load_pot.wait()
    for l in range(L):
        inside(0, l)
    for k in range(STEPS):
        for l in range(L):
            edges(k, l)
            for copy in halo(k + 1, l):
                copy.start()
            if k > 0:
                inside(k, l)
            if k == STEPS - 1:
                regroup_start(0, l)
    result = pltpu.make_async_copy(e.at[STEPS, :, inner], f_out, out_sem)
    result.start()
    for l in range(L):
        inside(STEPS, l)
    for l in range(L):
        edges(STEPS, l)
        regroup_start(1, l)

    def correlate():
        regroup_own(0)
        regroup_own(1)
        regroup_arrive(0)
        fhi[...], flo[...] = halves_of(fall)
        gram = product(fhi[...], flo[...])
        for g in range(nb):
            part[g, 0:L, :] = gram[g * L:(g + 1) * L]
        regroup_arrive(1)
        proj = product(*halves_of(iall))
        for g in range(nb):
            part[g, L:2 * L, :] = proj[g * L:(g + 1) * L]

    if active == nb:
        correlate()
    else:
        pl.when(b < active)(correlate)

        @pl.when(b >= active)
        def _():
            part[...] = jnp.zeros_like(part)

    def row(d):
        peer = lax.rem(b + d, nb)
        return pltpu.make_async_remote_copy(
            src_ref=part.at[peer],
            dst_ref=rb.at[b],
            send_sem=row_send.at[d],
            recv_sem=row_recv.at[d],
            device_id={"band": peer},
            device_id_type=MESH,
        )

    def each_row(action):
        def step(d, carry):
            action(row(d))
            return carry

        lax.fori_loop(1, nb, step, 0)

    each_row(lambda copy: copy.start())
    rb[b] = part[b]
    each_row(lambda copy: copy.wait_recv())
    rs[s] = jnp.sum(rb[...], axis=0)

    def across(d):
        return pltpu.make_async_remote_copy(
            src_ref=rs.at[s],
            dst_ref=rs.at[s],
            send_sem=slab_send.at[d],
            recv_sem=slab_recv.at[d],
            device_id={"slab": lax.rem(s + d, ns)},
            device_id_type=MESH,
        )

    for d in range(1, ns):
        across(d).start()
    for d in range(1, ns):
        across(d).wait_recv()
    total = rs[0]
    for other in range(1, ns):
        total = total + rs[other]
    cp_out[...] = total
    for d in range(1, ns):
        across(d).wait_send()
    each_row(lambda copy: copy.wait_send())
    for k in range(STEPS + 1):
        for l in range(L):
            for copy in halo(k, l):
                copy.wait_send()
    regroup_sent(0)
    regroup_sent(1)
    result.wait()


def finish(f, cp, f_out, c_out, p_out, sem):
    L = c_out.shape[0]
    copy = pltpu.make_async_copy(f, f_out, sem)
    copy.start()
    c_out[...] = cp[:L]
    p_out[...] = cp[L:]
    copy.wait()


def body(bands, potential):
    L, nz, ny, nx = bands.shape
    nb, ns = lax.axis_size("band"), lax.axis_size("slab")
    rows = nz * ny
    tiles = rows // 8
    each = -(-tiles // nb)
    while tiles % each:
        each += 1
    chunk = each * 8
    active = rows // chunk
    dims = (nb, ns, L, nz, ny, chunk, active, 1.0 / (rows * ns * nx))
    f32 = jnp.float32
    anywhere, vmem = pl.BlockSpec(memory_space=pl.ANY), pl.BlockSpec(memory_space=pltpu.VMEM)
    dma = pltpu.SemaphoreType.DMA
    f, cp = pl.pallas_call(
        functools.partial(kernel, dims),
        out_shape=(
            jax.ShapeDtypeStruct((L, rows, nx), f32),
            jax.ShapeDtypeStruct((2 * L, nb * L), f32),
        ),
        in_specs=[anywhere, anywhere],
        out_specs=(anywhere, vmem),
        scratch_shapes=[
            pltpu.VMEM((STEPS + 1, L, (nz + 4) * ny, nx), f32),
            pltpu.VMEM((rows, nx), f32),
            pltpu.VMEM((L, rows, nx), f32),
            pltpu.VMEM((nb, L, chunk, nx), f32),
            pltpu.VMEM((nb, L, chunk, nx), f32),
            pltpu.VMEM((nb * L, chunk * nx), jnp.bfloat16),
            pltpu.VMEM((nb * L, chunk * nx), jnp.bfloat16),
            pltpu.VMEM((nb, 2 * L, nb * L), f32),
            pltpu.VMEM((nb, 2 * L, nb * L), f32),
            pltpu.VMEM((ns, 2 * L, nb * L), f32),
            dma((STEPS + 1, L, 2)), dma((STEPS + 1, L, 2)),
            dma((2,)), dma,
            dma((2, nb, L)), dma((2, nb, L)),
            dma((nb,)), dma((nb,)),
            dma((ns,)), dma((ns,)),
        ],
        compiler_params=pltpu.CompilerParams(
            collective_id=0, has_side_effects=True, vmem_limit_bytes=60 * 1024 * 1024
        ),
    )(bands.reshape(L, rows, nx), potential.reshape(rows, nx))
    f, c, p = pl.pallas_call(
        finish,
        out_shape=(
            jax.ShapeDtypeStruct((L, rows, nx), f32),
            jax.ShapeDtypeStruct((L, nb * L), f32),
            jax.ShapeDtypeStruct((L, nb * L), f32),
        ),
        in_specs=[anywhere, vmem],
        out_specs=(anywhere, vmem, vmem),
        scratch_shapes=[dma],
        compiler_params=pltpu.CompilerParams(vmem_limit_bytes=60 * 1024 * 1024),
    )(f, cp)
    return f.reshape(L, nz, ny, nx), c, p


def solution(mesh):
    in_specs = (P("band", "slab", None, None), P("slab", None, None))
    out_specs = (P("band", "slab", None, None), P("band", None), P("band", None))
    return jax.shard_map(body, mesh=mesh, in_specs=in_specs, out_specs=out_specs, check_vma=False)
```

```python
import functools

import jax
import jax.numpy as jnp
from jax import lax
from jax.experimental import pallas as pl
from jax.experimental.pallas import tpu as pltpu
from jax.sharding import PartitionSpec as P

centre = 4.5
half = 3.5
MESH = pl.DeviceIdType.MESH
STEPS = 4


def shifted(v, axis):
    n = v.shape[axis]
    near = pltpu.roll(v, 1, axis) + pltpu.roll(v, n - 1, axis)
    far = pltpu.roll(v, 2, axis) + pltpu.roll(v, n - 2, axis)
    return near, far


def kernel(
    dims, bands, pot, f_out, cp_out,
    e, vbuf, img, fall, iall, fhi, flo, part, rb, rs,
    halo_send, halo_recv, load_sem, out_sem, gram_send, gram_recv,
    row_send, row_recv, slab_send, slab_recv,
):
    nb, ns, L, nz, ny, chunk, active, volume = dims
    b, s = lax.axis_index("band"), lax.axis_index("slab")
    up, down = lax.rem(s + 1, ns), lax.rem(s + ns - 1, ns)
    inner = pl.ds(2 * ny, nz * ny)

    load = pltpu.make_async_copy(bands, e.at[0, :, inner], load_sem.at[0])
    load.start()
    load_pot = pltpu.make_async_copy(pot, vbuf, load_sem.at[1])
    load_pot.start()

    barrier = pltpu.get_barrier_semaphore()

    def greet_band(d, carry):
        pl.semaphore_signal(
            barrier, inc=1, device_id={"band": lax.rem(b + d, nb)}, device_id_type=MESH
        )
        return carry

    lax.fori_loop(1, nb, greet_band, 0)
    for d in range(1, ns):
        pl.semaphore_signal(
            barrier, inc=1, device_id={"slab": lax.rem(s + d, ns)}, device_id_type=MESH
        )
    pl.semaphore_wait(barrier, nb - 1 + ns - 1)

    def halo(k, l):
        if k == 0:
            low, high = bands.at[l, pl.ds(0, 2 * ny)], bands.at[l, pl.ds((nz - 2) * ny, 2 * ny)]
        else:
            low, high = e.at[k, l, pl.ds(2 * ny, 2 * ny)], e.at[k, l, pl.ds(nz * ny, 2 * ny)]
        return (
            pltpu.make_async_remote_copy(
                src_ref=low,
                dst_ref=e.at[k, l, pl.ds((nz + 2) * ny, 2 * ny)],
                send_sem=halo_send.at[k, l, 0],
                recv_sem=halo_recv.at[k, l, 0],
                device_id={"slab": down},
                device_id_type=MESH,
            ),
            pltpu.make_async_remote_copy(
                src_ref=high,
                dst_ref=e.at[k, l, pl.ds(0, 2 * ny)],
                send_sem=halo_send.at[k, l, 1],
                recv_sem=halo_recv.at[k, l, 1],
                device_id={"slab": up},
                device_id_type=MESH,
            ),
        )

    def plane(k, l, z):
        def rows(offset):
            start = (z + 2 + offset) * ny
            return pl.ds(start if isinstance(z, int) else pl.multiple_of(start, 8), ny)

        here = pl.ds(z * ny if isinstance(z, int) else pl.multiple_of(z * ny, 8), ny)
        scale = 1.0 if k == STEPS else (1.0 if k == 0 else 2.0) / half
        shift = 3.75 if k == STEPS else 3.75 - centre
        diagonal = (vbuf[here, :] + shift) * scale
        v = e[k, l, rows(0), :]
        near = e[k, l, rows(-1), :] + e[k, l, rows(1), :]
        far = e[k, l, rows(-2), :] + e[k, l, rows(2), :]
        for axis in (0, 1):
            n1, n2 = shifted(v, axis)
            near = near + n1
            far = far + n2
        value = diagonal * v - (scale * 2.0 / 3.0) * near + (scale / 24.0) * far
        if k == STEPS:
            img[l, here, :] = value
        else:
            if k > 0:
                value = value - e[k - 1, l, rows(0), :]
            e[k + 1, l, rows(0), :] = value

    def inside(k, l):
        for z in range(2, nz - 2):
            plane(k, l, z)

    def edges(k, l):
        for copy in halo(k, l):
            copy.wait_recv()
        for z in (0, 1, nz - 2, nz - 1):
            plane(k, l, z)

    def partner(d):
        if nb & (nb - 1):
            return lax.rem(b + d, nb)
        peer, bit = 0, 1
        while bit < nb:
            peer = peer + lax.rem(lax.div(b, bit) + lax.div(nb - d, bit), 2) * bit
            bit *= 2
        return peer

    def regroup(which, d, l):
        peer = partner(d)
        cells = pl.multiple_of(peer * chunk, 8)
        if which == 0:
            src = e.at[STEPS, l, pl.ds(2 * ny + cells, chunk)]
        else:
            src = img.at[l, pl.ds(cells, chunk)]
        return pltpu.make_async_remote_copy(
            src_ref=src,
            dst_ref=(fall, iall)[which].at[b, l],
            send_sem=gram_send.at[which, d, l],
            recv_sem=gram_recv.at[which, d, l],
            device_id={"band": peer},
            device_id_type=MESH,
        ), peer

    def when_active(peer, action):
        if active == nb:
            action()
        else:
            pl.when(peer < active)(action)

    def regroup_start(which, l):
        def step(d, carry):
            copy, peer = regroup(which, d, l)
            when_active(peer, copy.start)
            return carry

        lax.fori_loop(1, nb, step, 0)

    def regroup_sent(which):
        def step(d, carry):
            for l in range(L):
                copy, peer = regroup(which, d, l)
                when_active(peer, copy.wait_send)
            return carry

        lax.fori_loop(1, nb, step, 0)

    def regroup_own(which):
        mine = pl.multiple_of(b * chunk, 8)
        if which == 0:
            fall[b] = e[STEPS, :, pl.ds(2 * ny + mine, chunk), :]
        else:
            iall[b] = img[:, pl.ds(mine, chunk), :]

    def regroup_arrive(which):
        def step(d, carry):
            for l in range(L):
                regroup(which, d, l)[0].wait_recv()
            return carry

        lax.fori_loop(1, nb, step, 0)

    def halves_of(ref):
        flat = ref.reshape(nb * L * chunk, ref.shape[-1])
        whole = jnp.concatenate(
            [flat[pl.ds(r, nb * L, stride=chunk), :] for r in range(chunk)], axis=1
        )
        high = whole.astype(jnp.bfloat16)
        return high, (whole - high.astype(jnp.float32)).astype(jnp.bfloat16)

    def product(high, low):
        both = jnp.concatenate([high, low], axis=0)
        out = sum(
            lax.dot_general(
                both, other[...], (((1,), (1,)), ((), ())),
                preferred_element_type=jnp.float32,
            )
            for other in (flo, fhi)
        )
        return (out[nb * L:] + out[:nb * L]) * volume

    for l in range(L):
        for copy in halo(0, l):
            copy.start()
    load.wait()
    load_pot.wait()
    for first in range(0, L, 2):
        group = range(first, min(first + 2, L))
        for l in group:
            inside(0, l)
        for k in range(STEPS):
            for l in group:
                edges(k, l)
                for copy in halo(k + 1, l):
                    copy.start()
                if k > 0:
                    inside(k, l)
                if k == STEPS - 1:
                    regroup_start(0, l)
        for l in group:
            inside(STEPS, l)
        for l in group:
            edges(STEPS, l)
            regroup_start(1, l)
    result = pltpu.make_async_copy(e.at[STEPS, :, inner], f_out, out_sem)
    result.start()

    def correlate():
        regroup_own(0)
        regroup_own(1)
        regroup_arrive(0)
        fhi[...], flo[...] = halves_of(fall)
        gram = product(fhi[...], flo[...])
        for g in range(nb):
            part[g, 0:L, :] = gram[g * L:(g + 1) * L]
        regroup_arrive(1)
        proj = product(*halves_of(iall))
        for g in range(nb):
            part[g, L:2 * L, :] = proj[g * L:(g + 1) * L]

    if active == nb:
        correlate()
    else:
        pl.when(b < active)(correlate)

        @pl.when(b >= active)
        def _():
            part[...] = jnp.zeros_like(part)

    def row(d):
        peer = lax.rem(b + d, nb)
        return pltpu.make_async_remote_copy(
            src_ref=part.at[peer],
            dst_ref=rb.at[b],
            send_sem=row_send.at[d],
            recv_sem=row_recv.at[d],
            device_id={"band": peer},
            device_id_type=MESH,
        )

    def each_row(action):
        def step(d, carry):
            action(row(d))
            return carry

        lax.fori_loop(1, nb, step, 0)

    each_row(lambda copy: copy.start())
    rb[b] = part[b]
    each_row(lambda copy: copy.wait_recv())
    rs[s] = jnp.sum(rb[...], axis=0)

    def across(d):
        return pltpu.make_async_remote_copy(
            src_ref=rs.at[s],
            dst_ref=rs.at[s],
            send_sem=slab_send.at[d],
            recv_sem=slab_recv.at[d],
            device_id={"slab": lax.rem(s + d, ns)},
            device_id_type=MESH,
        )

    for d in range(1, ns):
        across(d).start()
    for d in range(1, ns):
        across(d).wait_recv()
    total = rs[0]
    for other in range(1, ns):
        total = total + rs[other]
    cp_out[...] = total
    for d in range(1, ns):
        across(d).wait_send()
    each_row(lambda copy: copy.wait_send())
    for k in range(STEPS + 1):
        for l in range(L):
            for copy in halo(k, l):
                copy.wait_send()
    regroup_sent(0)
    regroup_sent(1)
    result.wait()


def finish(f, cp, f_out, c_out, p_out, held, loaded, stored):
    L = c_out.shape[0]
    loads = [pltpu.make_async_copy(f.at[l], held.at[l], loaded.at[l]) for l in range(L)]
    stores = [pltpu.make_async_copy(held.at[l], f_out.at[l], stored.at[l]) for l in range(L)]
    for load in loads:
        load.start()
    c_out[...] = cp[:L]
    p_out[...] = cp[L:]
    for load, store in zip(loads, stores):
        load.wait()
        store.start()
    for store in stores:
        store.wait()


def body(bands, potential):
    L, nz, ny, nx = bands.shape
    nb, ns = lax.axis_size("band"), lax.axis_size("slab")
    rows = nz * ny
    tiles = rows // 8
    each = -(-tiles // nb)
    while tiles % each:
        each += 1
    chunk = each * 8
    active = rows // chunk
    dims = (nb, ns, L, nz, ny, chunk, active, 1.0 / (rows * ns * nx))
    f32 = jnp.float32
    anywhere, vmem = pl.BlockSpec(memory_space=pl.ANY), pl.BlockSpec(memory_space=pltpu.VMEM)
    dma = pltpu.SemaphoreType.DMA
    f, cp = pl.pallas_call(
        functools.partial(kernel, dims),
        out_shape=(
            jax.ShapeDtypeStruct((L, rows, nx), f32),
            jax.ShapeDtypeStruct((2 * L, nb * L), f32),
        ),
        in_specs=[anywhere, anywhere],
        out_specs=(anywhere, vmem),
        scratch_shapes=[
            pltpu.VMEM((STEPS + 1, L, (nz + 4) * ny, nx), f32),
            pltpu.VMEM((rows, nx), f32),
            pltpu.VMEM((L, rows, nx), f32),
            pltpu.VMEM((nb, L, chunk, nx), f32),
            pltpu.VMEM((nb, L, chunk, nx), f32),
            pltpu.VMEM((nb * L, chunk * nx), jnp.bfloat16),
            pltpu.VMEM((nb * L, chunk * nx), jnp.bfloat16),
            pltpu.VMEM((nb, 2 * L, nb * L), f32),
            pltpu.VMEM((nb, 2 * L, nb * L), f32),
            pltpu.VMEM((ns, 2 * L, nb * L), f32),
            dma((STEPS + 1, L, 2)), dma((STEPS + 1, L, 2)),
            dma((2,)), dma,
            dma((2, nb, L)), dma((2, nb, L)),
            dma((nb,)), dma((nb,)),
            dma((ns,)), dma((ns,)),
        ],
        compiler_params=pltpu.CompilerParams(
            collective_id=0, has_side_effects=True, vmem_limit_bytes=60 * 1024 * 1024
        ),
    )(bands.reshape(L, rows, nx), potential.reshape(rows, nx))
    f, c, p = pl.pallas_call(
        finish,
        out_shape=(
            jax.ShapeDtypeStruct((L, rows, nx), f32),
            jax.ShapeDtypeStruct((L, nb * L), f32),
            jax.ShapeDtypeStruct((L, nb * L), f32),
        ),
        in_specs=[anywhere, vmem],
        out_specs=(anywhere, vmem, vmem),
        scratch_shapes=[pltpu.VMEM((L, rows, nx), f32), dma((L,)), dma((L,))],
        compiler_params=pltpu.CompilerParams(vmem_limit_bytes=60 * 1024 * 1024),
    )(f, cp)
    return f.reshape(L, nz, ny, nx), c, p


def solution(mesh):
    in_specs = (P("band", "slab", None, None), P("slab", None, None))
    out_specs = (P("band", "slab", None, None), P("band", None), P("band", None))
    return jax.shard_map(body, mesh=mesh, in_specs=in_specs, out_specs=out_specs, check_vma=False)
```

```python
import functools

import jax
import jax.numpy as jnp
from jax import lax
from jax.experimental import pallas as pl
from jax.experimental.pallas import tpu as pltpu
from jax.sharding import PartitionSpec as P

centre = 4.5
half = 3.5
MESH = pl.DeviceIdType.MESH
STEPS = 4


def shifted(v, axis):
    n = v.shape[axis]
    near = pltpu.roll(v, 1, axis) + pltpu.roll(v, n - 1, axis)
    far = pltpu.roll(v, 2, axis) + pltpu.roll(v, n - 2, axis)
    return near, far


def kernel(
    dims, bands, pot, f_out, c_out, p_out,
    e, vbuf, vt, turned, tails, blocks, ends, left, part, rb, rs,
    halo_send, halo_recv, load_sem, out_sem,
    early_send, early_recv, late_send, late_recv, end_send, end_recv,
    row_send, row_recv, slab_send, slab_recv,
):
    nb, ns, L, nz, ny, nx, chunk, active, count, volume = dims
    J = count // 128
    b, s = lax.axis_index("band"), lax.axis_index("slab")
    up, down = lax.rem(s + 1, ns), lax.rem(s + ns - 1, ns)
    inner = pl.ds(2 * ny, nz * ny)

    load = pltpu.make_async_copy(bands, e.at[0, :, inner], load_sem.at[0])
    load.start()
    load_pot = pltpu.make_async_copy(pot, vbuf.at[pl.ds(0, nz * ny)], load_sem.at[1])
    load_pot.start()

    barrier = pltpu.get_barrier_semaphore()

    def greet_band(d, carry):
        pl.semaphore_signal(
            barrier, inc=1, device_id={"band": lax.rem(b + d, nb)}, device_id_type=MESH
        )
        return carry

    lax.fori_loop(1, nb, greet_band, 0)
    for d in range(1, ns):
        pl.semaphore_signal(
            barrier, inc=1, device_id={"slab": lax.rem(s + d, ns)}, device_id_type=MESH
        )
    pl.semaphore_wait(barrier, nb - 1 + ns - 1)

    vbuf[nz * ny:count, :] = jnp.zeros((count - nz * ny, nx), jnp.float32)
    spare = 2 * ny + count - (nz + 4) * ny
    if spare > 0:
        e[STEPS, :, (nz + 4) * ny:2 * ny + count, :] = jnp.zeros((L, spare, nx), jnp.float32)

    def halo(k, l):
        if k == 0:
            low, high = bands.at[l, pl.ds(0, 2 * ny)], bands.at[l, pl.ds((nz - 2) * ny, 2 * ny)]
        else:
            low, high = e.at[k, l, pl.ds(2 * ny, 2 * ny)], e.at[k, l, pl.ds(nz * ny, 2 * ny)]
        copies = (
            pltpu.make_async_remote_copy(
                src_ref=low,
                dst_ref=e.at[k, l, pl.ds((nz + 2) * ny, 2 * ny)],
                send_sem=halo_send.at[k, l, 0],
                recv_sem=halo_recv.at[k, l, 0],
                device_id={"slab": down},
                device_id_type=MESH,
            ),
            pltpu.make_async_remote_copy(
                src_ref=high,
                dst_ref=e.at[k, l, pl.ds(0, 2 * ny)],
                send_sem=halo_send.at[k, l, 1],
                recv_sem=halo_recv.at[k, l, 1],
                device_id={"slab": up},
                device_id_type=MESH,
            ),
        )
        return copies[:1] if k == STEPS else copies

    def plane(k, l, z):
        def rows(offset):
            start = (z + 2 + offset) * ny
            return pl.ds(start if isinstance(z, int) else pl.multiple_of(start, 8), ny)

        here = pl.ds(z * ny if isinstance(z, int) else pl.multiple_of(z * ny, 8), ny)
        scale = (1.0 if k == 0 else 2.0) / half
        diagonal = (vbuf[here, :] + (3.75 - centre)) * scale
        v = e[k, l, rows(0), :]
        near = e[k, l, rows(-1), :] + e[k, l, rows(1), :]
        far = e[k, l, rows(-2), :] + e[k, l, rows(2), :]
        for axis in (0, 1):
            n1, n2 = shifted(v, axis)
            near = near + n1
            far = far + n2
        value = diagonal * v - (scale * 2.0 / 3.0) * near + (scale / 24.0) * far
        if k > 0:
            value = value - e[k - 1, l, rows(0), :]
        e[k + 1, l, rows(0), :] = value

    def inside(k, l):
        for z in range(2, nz - 2):
            plane(k, l, z)

    def edges(k, l):
        for copy in halo(k, l):
            copy.wait_recv()
        for z in (0, 1, nz - 2, nz - 1):
            plane(k, l, z)

    def send(src, dst, sent, arrived, peer):
        return pltpu.make_async_remote_copy(
            src_ref=src,
            dst_ref=dst,
            send_sem=sent,
            recv_sem=arrived,
            device_id={"band": peer},
            device_id_type=MESH,
        )

    def cells_of(peer):
        return pl.ds(pl.multiple_of(peer * chunk, 8), chunk)

    def early(j, l):
        return lambda d, peer: send(
            turned.at[j, l, cells_of(peer)], blocks.at[j, b, l],
            early_send.at[j, l, d], early_recv.at[j, l, d], peer,
        )

    def late(j):
        return lambda d, peer: send(
            turned.at[j, :, cells_of(peer)], blocks.at[j, b],
            late_send.at[j, d], late_recv.at[j, d], peer,
        )

    def end(d, peer):
        return send(tails.at[peer], ends.at[:, b], end_send.at[d], end_recv.at[d], peer)

    def when_active(peer, action):
        if active == nb:
            action()
        else:
            pl.when(peer < active)(action)

    def each_peer(copies, action, everywhere=False):
        def step(d, carry):
            peer = lax.rem(b + d, nb)
            for copy in copies:
                if everywhere:
                    action(copy(d, peer))
                else:
                    when_active(peer, lambda copy=copy: action(copy(d, peer)))
            return carry

        lax.fori_loop(1, nb, step, 0)

    soon = [j for j in range(J) if 128 * (j + 1) <= nz * ny]
    later = [j for j in range(J) if j not in soon]
    groups = [early(j, l) for j in soon for l in range(L)] + [late(j) for j in later] + [end]

    def turn(j, l):
        turned[j, l] = e[STEPS, l, 2 * ny + 128 * j:2 * ny + 128 * (j + 1), :].T

    def correlate():
        own = cells_of(b)
        for j in range(J):
            blocks[j, b] = turned[j, :, own, :]
        ends[:, b] = tails[b]
        each_peer(groups, lambda copy: copy.wait_recv(), everywhere=True)
        flat = blocks.reshape(J * nb * L * chunk, 128)
        flat_ends = ends.reshape(J * nb * 2 * L, 128)

        def line(r):
            if r < chunk:
                pieces = [
                    flat[pl.ds(j * nb * L * chunk + r, nb * L, stride=chunk), :] for j in range(J)
                ]
            else:
                pieces = [
                    flat_ends[pl.ds(j * nb * 2 * L + r - chunk, nb * L, stride=2), :]
                    for j in range(J)
                ]
            return jnp.concatenate(pieces, axis=1)

        lane = lax.broadcasted_iota(jnp.int32, (nb * L, count), 1)
        y = lane
        for z in range(1, nz + 2):
            y = y - jnp.where(lane >= z * ny, ny, 0)
        inside_slab = lane < nz * ny
        mine = jnp.concatenate([vt[j, own, :] for j in range(J)], axis=1)

        def ahead(x, n):
            return pltpu.roll(x, count - n, 1)

        def split(x):
            high = x.astype(jnp.bfloat16)
            return high, (x - high.astype(jnp.float32)).astype(jnp.bfloat16)

        N = nb * L
        lines = [line(0), line(1)]
        for r in range(chunk):
            lines.append(line(r + 2))
            x = lines[r]
            near = lines[r + 1] + ahead(x, ny)
            near = near + jnp.where(y < ny - 1, ahead(x, 1), pltpu.roll(x, ny - 1, 1))
            far = lines[r + 2] + ahead(x, 2 * ny)
            far = far + jnp.where(y < ny - 2, ahead(x, 2), pltpu.roll(x, ny - 2, 1))
            w = (0.5 * mine[r:r + 1, :] + 1.875) * x - (2.0 / 3.0) * near + (1.0 / 24.0) * far
            x = jnp.where(inside_slab, x, 0.0)
            w = jnp.where(inside_slab, w, 0.0)
            place = pl.ds(r * count, count)
            xh, xl = split(x)
            wh, wl = split(w)
            for i, piece in enumerate((xh, xl, wh, wl)):
                left[i * N:(i + 1) * N, place] = piece
        out = sum(
            lax.dot_general(
                left[...], left[i * N:(i + 1) * N, :], (((1,), (1,)), ((), ())),
                preferred_element_type=jnp.float32,
            )
            for i in (1, 0)
        ) * volume
        gram = out[N:2 * N] + out[:N]
        skew = out[3 * N:] + out[2 * N:3 * N]
        proj = skew + skew.T
        for g in range(nb):
            part[g, 0:L, :] = gram[g * L:(g + 1) * L]
            part[g, L:2 * L, :] = proj[g * L:(g + 1) * L]

    for l in range(L):
        for copy in halo(0, l):
            copy.start()
    load.wait()
    load_pot.wait()
    for l in range(L):
        inside(0, l)
    for k in range(STEPS):
        for l in range(L):
            edges(k, l)
            for copy in halo(k + 1, l):
                copy.start()
            if k > 0:
                inside(k, l)
            if k == STEPS - 1:
                for j in soon:
                    turn(j, l)
                each_peer([early(j, l) for j in soon], lambda copy: copy.start())
    result = pltpu.make_async_copy(e.at[STEPS, :, inner], f_out, out_sem)
    result.start()
    for l in range(L):
        for copy in halo(STEPS, l):
            copy.wait_recv()
        for j in later:
            turn(j, l)
    each_peer([late(j) for j in later], lambda copy: copy.start())
    for g in range(active):
        after = (g + 1) * chunk % nx
        for j in range(J):
            for l in range(L):
                tails[g, j, 2 * l:2 * l + 2, :] = turned[j, l, after:after + 2, :]
    each_peer([end], lambda copy: copy.start())
    for j in range(J):
        vt[j] = vbuf[128 * j:128 * (j + 1), :].T

    if active == nb:
        correlate()
    else:
        pl.when(b < active)(correlate)

        @pl.when(b >= active)
        def _():
            part[...] = jnp.zeros_like(part)

    def row(d):
        peer = lax.rem(b + d, nb)
        return pltpu.make_async_remote_copy(
            src_ref=part.at[peer],
            dst_ref=rb.at[b],
            send_sem=row_send.at[d],
            recv_sem=row_recv.at[d],
            device_id={"band": peer},
            device_id_type=MESH,
        )

    def each_row(action):
        def step(d, carry):
            action(row(d))
            return carry

        lax.fori_loop(1, nb, step, 0)

    each_row(lambda copy: copy.start())
    rb[b] = part[b]
    each_row(lambda copy: copy.wait_recv())
    rs[s] = jnp.sum(rb[...], axis=0)

    def across(d):
        return pltpu.make_async_remote_copy(
            src_ref=rs.at[s],
            dst_ref=rs.at[s],
            send_sem=slab_send.at[d],
            recv_sem=slab_recv.at[d],
            device_id={"slab": lax.rem(s + d, ns)},
            device_id_type=MESH,
        )

    for d in range(1, ns):
        across(d).start()
    for d in range(1, ns):
        across(d).wait_recv()
    total = rs[0]
    for other in range(1, ns):
        total = total + rs[other]
    c_out[...] = total[:L]
    p_out[...] = total[L:]
    for d in range(1, ns):
        across(d).wait_send()
    each_row(lambda copy: copy.wait_send())
    for k in range(STEPS + 1):
        for l in range(L):
            for copy in halo(k, l):
                copy.wait_send()
    each_peer(groups, lambda copy: copy.wait_send())
    result.wait()


def body(bands, potential):
    L, nz, ny, nx = bands.shape
    nb, ns = lax.axis_size("band"), lax.axis_size("slab")
    rows = nz * ny
    tiles = nx // 8
    each = -(-tiles // nb)
    while tiles % each:
        each += 1
    chunk = each * 8
    active = nx // chunk
    count = -(-(nz + 2) * ny // 128) * 128
    J = count // 128
    held = max((nz + 4) * ny, 2 * ny + count)
    dims = (nb, ns, L, nz, ny, nx, chunk, active, count, 1.0 / (rows * ns * nx))
    f32 = jnp.float32
    anywhere, vmem = pl.BlockSpec(memory_space=pl.ANY), pl.BlockSpec(memory_space=pltpu.VMEM)
    dma = pltpu.SemaphoreType.DMA
    f, c, p = pl.pallas_call(
        functools.partial(kernel, dims),
        out_shape=(
            jax.ShapeDtypeStruct((L, rows, nx), f32),
            jax.ShapeDtypeStruct((L, nb * L), f32),
            jax.ShapeDtypeStruct((L, nb * L), f32),
        ),
        in_specs=[anywhere, anywhere],
        out_specs=(anywhere, vmem, vmem),
        scratch_shapes=[
            pltpu.VMEM((STEPS + 1, L, held, nx), f32),
            pltpu.VMEM((count, nx), f32),
            pltpu.VMEM((J, nx, 128), f32),
            pltpu.VMEM((J, L, nx, 128), f32),
            pltpu.VMEM((nb, J, 2 * L, 128), f32),
            pltpu.VMEM((J, nb, L, chunk, 128), f32),
            pltpu.VMEM((J, nb, 2 * L, 128), f32),
            pltpu.VMEM((4 * nb * L, chunk * count), jnp.bfloat16),
            pltpu.VMEM((nb, 2 * L, nb * L), f32),
            pltpu.VMEM((nb, 2 * L, nb * L), f32),
            pltpu.VMEM((ns, 2 * L, nb * L), f32),
            dma((STEPS + 1, L, 2)), dma((STEPS + 1, L, 2)),
            dma((2,)), dma,
            dma((J, L, nb)), dma((J, L, nb)),
            dma((J, nb)), dma((J, nb)),
            dma((nb,)), dma((nb,)),
            dma((nb,)), dma((nb,)),
            dma((ns,)), dma((ns,)),
        ],
        compiler_params=pltpu.CompilerParams(
            collective_id=0, has_side_effects=True, vmem_limit_bytes=60 * 1024 * 1024
        ),
    )(bands.reshape(L, rows, nx), potential.reshape(rows, nx))
    return f.reshape(L, nz, ny, nx), c, p


def solution(mesh):
    in_specs = (P("band", "slab", None, None), P("slab", None, None))
    out_specs = (P("band", "slab", None, None), P("band", None), P("band", None))
    return jax.shard_map(body, mesh=mesh, in_specs=in_specs, out_specs=out_specs, check_vma=False)
```

```python
import functools

import jax
import jax.numpy as jnp
from jax import lax
from jax.experimental import pallas as pl
from jax.experimental.pallas import tpu as pltpu
from jax.sharding import PartitionSpec as P

centre = 4.5
half = 3.5
MESH = pl.DeviceIdType.MESH
STEPS = 4
BELOW, ABOVE = 4, 6


def shifted(v, axis):
    n = v.shape[axis]
    near = pltpu.roll(v, 1, axis) + pltpu.roll(v, n - 1, axis)
    far = pltpu.roll(v, 2, axis) + pltpu.roll(v, n - 2, axis)
    return near, far


def kernel(
    dims, bands, pot, f_out, c_out, p_out,
    e, vbuf, vt, turned, tails, blocks, ends, left, part, rb, rs,
    halo_send, halo_recv, load_sem, out_sem,
    block_send, block_recv, end_send, end_recv,
    row_send, row_recv, slab_send, slab_recv,
):
    nb, ns, L, nz, ny, nx, chunk, active, count, volume = dims
    J = count // 128
    b, s = lax.axis_index("band"), lax.axis_index("slab")
    up, down = lax.rem(s + 1, ns), lax.rem(s + ns - 1, ns)
    inner = pl.ds(BELOW * ny, nz * ny)
    base = BELOW * ny

    load = pltpu.make_async_copy(bands, e.at[0, :, inner], load_sem.at[0])
    load.start()
    load_pot = pltpu.make_async_copy(pot, vbuf.at[inner], load_sem.at[1])
    load_pot.start()

    barrier = pltpu.get_barrier_semaphore()

    def greet_band(d, carry):
        pl.semaphore_signal(
            barrier, inc=1, device_id={"band": lax.rem(b + d, nb)}, device_id_type=MESH
        )
        return carry

    lax.fori_loop(1, nb, greet_band, 0)
    for d in range(1, ns):
        pl.semaphore_signal(
            barrier, inc=1, device_id={"slab": lax.rem(s + d, ns)}, device_id_type=MESH
        )
    pl.semaphore_wait(barrier, nb - 1 + ns - 1)

    stale = base + (nz + 2) * ny
    if base + count > stale:
        spare = base + count - stale
        e[STEPS, :, stale:base + count, :] = jnp.zeros((L, spare, nx), jnp.float32)

    def pushed(src, dst, order, device):
        return pltpu.make_async_remote_copy(
            src_ref=src,
            dst_ref=dst,
            send_sem=halo_send.at[order],
            recv_sem=halo_recv.at[order],
            device_id={"slab": device},
            device_id_type=MESH,
        )

    def span(start, size):
        return pl.ds(start * ny, size * ny)

    def halo(stage, l):
        if stage == 0:
            low, high = bands.at[l, span(0, ABOVE)], bands.at[l, span(nz - BELOW, BELOW)]
        else:
            low, high = e.at[2, l, span(BELOW, ABOVE)], e.at[2, l, span(nz, BELOW)]
        k, order = 2 * stage, 2 * (stage * L + l)
        return (
            pushed(low, e.at[k, l, span(BELOW + nz, ABOVE)], order, down),
            pushed(high, e.at[k, l, span(0, BELOW)], order + 1, up),
        )

    def potential_halo():
        order = 4 * L
        low, high = pot.at[span(0, ABOVE - 2)], pot.at[span(nz - BELOW + 2, BELOW - 2)]
        return (
            pushed(low, vbuf.at[span(BELOW + nz, ABOVE - 2)], order, down),
            pushed(high, vbuf.at[span(2, BELOW - 2)], order + 1, up),
        )

    def plane(k, l, z):
        def rows(offset):
            start = (z + BELOW + offset) * ny
            return slice(start, start + ny)

        scale = (1.0 if k == 0 else 2.0) / half
        diagonal = (vbuf[rows(0), :] + (3.75 - centre)) * scale
        v = e[k, l, rows(0), :]
        near = e[k, l, rows(-1), :] + e[k, l, rows(1), :]
        far = e[k, l, rows(-2), :] + e[k, l, rows(2), :]
        for axis in (0, 1):
            n1, n2 = shifted(v, axis)
            near = near + n1
            far = far + n2
        value = diagonal * v - (scale * 2.0 / 3.0) * near + (scale / 24.0) * far
        if k > 0:
            value = value - e[k - 1, l, rows(0), :]
        e[k + 1, l, rows(0), :] = value

    def first_half(k, l):
        for z in range(2, nz - 2):
            plane(k, l, z)

    def second_half(k, l, stop):
        for z in (*range(-2, 2), *range(nz - 2, nz + 4)):
            plane(k, l, z)
        for z in range(stop):
            plane(k + 1, l, z)

    def send(src, dst, sent, arrived, peer):
        return pltpu.make_async_remote_copy(
            src_ref=src,
            dst_ref=dst,
            send_sem=sent,
            recv_sem=arrived,
            device_id={"band": peer},
            device_id_type=MESH,
        )

    def cells_of(peer):
        return pl.ds(pl.multiple_of(peer * chunk, 8), chunk)

    def block(l):
        return lambda d, peer: send(
            turned.at[:, l, cells_of(peer)], blocks.at[:, b, l],
            block_send.at[l, d], block_recv.at[l, d], peer,
        )

    def end(d, peer):
        return send(tails.at[peer], ends.at[:, b], end_send.at[d], end_recv.at[d], peer)

    def when_active(peer, action):
        if active == nb:
            action()
        else:
            pl.when(peer < active)(action)

    def each_peer(copies, action, everywhere=False):
        def step(d, carry):
            peer = lax.rem(b + d, nb)
            for copy in copies:
                if everywhere:
                    action(copy(d, peer))
                else:
                    when_active(peer, lambda copy=copy: action(copy(d, peer)))
            return carry

        lax.fori_loop(1, nb, step, 0)

    groups = [block(l) for l in range(L)] + [end]

    def turn(j, l):
        turned[j, l] = e[STEPS, l, base + 128 * j:base + 128 * (j + 1), :].T

    def correlate():
        own = cells_of(b)
        for j in range(J):
            blocks[j, b] = turned[j, :, own, :]
        ends[:, b] = tails[b]
        each_peer(groups, lambda copy: copy.wait_recv(), everywhere=True)
        flat = blocks.reshape(J * nb * L * chunk, 128)
        flat_ends = ends.reshape(J * nb * 2 * L, 128)

        def line(r):
            if r < chunk:
                pieces = [
                    flat[pl.ds(j * nb * L * chunk + r, nb * L, stride=chunk), :] for j in range(J)
                ]
            else:
                pieces = [
                    flat_ends[pl.ds(j * nb * 2 * L + r - chunk, nb * L, stride=2), :]
                    for j in range(J)
                ]
            return jnp.concatenate(pieces, axis=1)

        lane = lax.broadcasted_iota(jnp.int32, (nb * L, count), 1)
        y = lane
        for z in range(1, nz + 2):
            y = y - jnp.where(lane >= z * ny, ny, 0)
        inside_slab = lane < nz * ny
        mine = jnp.concatenate([vt[j, own, :] for j in range(J)], axis=1)

        def ahead(x, n):
            return pltpu.roll(x, count - n, 1)

        def split(x):
            high = x.astype(jnp.bfloat16)
            return high, (x - high.astype(jnp.float32)).astype(jnp.bfloat16)

        N = nb * L
        lines = [line(0), line(1)]
        for r in range(chunk):
            lines.append(line(r + 2))
            x = lines[r]
            near = lines[r + 1] + ahead(x, ny)
            near = near + jnp.where(y < ny - 1, ahead(x, 1), pltpu.roll(x, ny - 1, 1))
            far = lines[r + 2] + ahead(x, 2 * ny)
            far = far + jnp.where(y < ny - 2, ahead(x, 2), pltpu.roll(x, ny - 2, 1))
            w = (0.5 * mine[r:r + 1, :] + 1.875) * x - (2.0 / 3.0) * near + (1.0 / 24.0) * far
            x = jnp.where(inside_slab, x, 0.0)
            w = jnp.where(inside_slab, w, 0.0)
            place = pl.ds(r * count, count)
            xh, xl = split(x)
            wh, wl = split(w)
            for i, piece in enumerate((xh, xl, wh, wl)):
                left[i * N:(i + 1) * N, place] = piece
        out = sum(
            lax.dot_general(
                left[...], left[i * N:(i + 1) * N, :], (((1,), (1,)), ((), ())),
                preferred_element_type=jnp.float32,
            )
            for i in (1, 0)
        ) * volume
        gram = out[N:2 * N] + out[:N]
        skew = out[3 * N:] + out[2 * N:3 * N]
        proj = skew + skew.T
        for g in range(nb):
            part[g, 0:L, :] = gram[g * L:(g + 1) * L]
            part[g, L:2 * L, :] = proj[g * L:(g + 1) * L]

    for copy in potential_halo():
        copy.start()
    for l in range(L):
        for copy in halo(0, l):
            copy.start()
    load.wait()
    load_pot.wait()
    for l in range(L):
        first_half(0, l)
    for copy in potential_halo():
        copy.wait_recv()
    for l in range(L):
        for copy in halo(0, l):
            copy.wait_recv()
        second_half(0, l, nz)
        for copy in halo(1, l):
            copy.start()
    for l in range(L):
        first_half(2, l)
    for j in range(J):
        vt[j] = vbuf[base + 128 * j:base + 128 * (j + 1), :].T
    for l in range(L):
        for copy in halo(1, l):
            copy.wait_recv()
        second_half(2, l, nz + 2)
        for j in range(J):
            turn(j, l)
        each_peer([block(l)], lambda copy: copy.start())
    result = pltpu.make_async_copy(e.at[STEPS, :, inner], f_out, out_sem)
    result.start()
    for g in range(active):
        after = (g + 1) * chunk % nx
        for j in range(J):
            for l in range(L):
                tails[g, j, 2 * l:2 * l + 2, :] = turned[j, l, after:after + 2, :]
    each_peer([end], lambda copy: copy.start())
    if active == nb:
        correlate()
    else:
        pl.when(b < active)(correlate)

        @pl.when(b >= active)
        def _():
            part[...] = jnp.zeros_like(part)

    def row(d):
        peer = lax.rem(b + d, nb)
        return pltpu.make_async_remote_copy(
            src_ref=part.at[peer],
            dst_ref=rb.at[b],
            send_sem=row_send.at[d],
            recv_sem=row_recv.at[d],
            device_id={"band": peer},
            device_id_type=MESH,
        )

    def each_row(action):
        def step(d, carry):
            action(row(d))
            return carry

        lax.fori_loop(1, nb, step, 0)

    each_row(lambda copy: copy.start())
    rb[b] = part[b]
    each_row(lambda copy: copy.wait_recv())
    rs[s] = jnp.sum(rb[...], axis=0)

    def across(d):
        return pltpu.make_async_remote_copy(
            src_ref=rs.at[s],
            dst_ref=rs.at[s],
            send_sem=slab_send.at[d],
            recv_sem=slab_recv.at[d],
            device_id={"slab": lax.rem(s + d, ns)},
            device_id_type=MESH,
        )

    for d in range(1, ns):
        across(d).start()
    for d in range(1, ns):
        across(d).wait_recv()
    total = rs[0]
    for other in range(1, ns):
        total = total + rs[other]
    c_out[...] = total[:L]
    p_out[...] = total[L:]
    for d in range(1, ns):
        across(d).wait_send()
    each_row(lambda copy: copy.wait_send())
    for copy in potential_halo():
        copy.wait_send()
    for stage in (0, 1):
        for l in range(L):
            for copy in halo(stage, l):
                copy.wait_send()
    each_peer(groups, lambda copy: copy.wait_send())
    result.wait()


def body(bands, potential):
    L, nz, ny, nx = bands.shape
    nb, ns = lax.axis_size("band"), lax.axis_size("slab")
    rows = nz * ny
    tiles = nx // 8
    each = -(-tiles // nb)
    while tiles % each:
        each += 1
    chunk = each * 8
    active = nx // chunk
    count = -(-(nz + 2) * ny // 128) * 128
    J = count // 128
    held = max((nz + BELOW + ABOVE) * ny, BELOW * ny + count)
    dims = (nb, ns, L, nz, ny, nx, chunk, active, count, 1.0 / (rows * ns * nx))
    f32 = jnp.float32
    anywhere, vmem = pl.BlockSpec(memory_space=pl.ANY), pl.BlockSpec(memory_space=pltpu.VMEM)
    dma = pltpu.SemaphoreType.DMA
    f, c, p = pl.pallas_call(
        functools.partial(kernel, dims),
        out_shape=(
            jax.ShapeDtypeStruct((L, rows, nx), f32),
            jax.ShapeDtypeStruct((L, nb * L), f32),
            jax.ShapeDtypeStruct((L, nb * L), f32),
        ),
        in_specs=[pl.BlockSpec(memory_space=pltpu.HBM)] * 2,
        out_specs=(anywhere, vmem, vmem),
        scratch_shapes=[
            pltpu.VMEM((STEPS + 1, L, held, nx), f32),
            pltpu.VMEM((held, nx), f32),
            pltpu.VMEM((J, nx, 128), f32),
            pltpu.VMEM((J, L, nx, 128), f32),
            pltpu.VMEM((nb, J, 2 * L, 128), f32),
            pltpu.VMEM((J, nb, L, chunk, 128), f32),
            pltpu.VMEM((J, nb, 2 * L, 128), f32),
            pltpu.VMEM((4 * nb * L, chunk * count), jnp.bfloat16),
            pltpu.VMEM((nb, 2 * L, nb * L), f32),
            pltpu.VMEM((nb, 2 * L, nb * L), f32),
            pltpu.VMEM((ns, 2 * L, nb * L), f32),
            dma((4 * L + 2,)), dma((4 * L + 2,)),
            dma((2,)), dma,
            dma((L, nb)), dma((L, nb)),
            dma((nb,)), dma((nb,)),
            dma((nb,)), dma((nb,)),
            dma((ns,)), dma((ns,)),
        ],
        compiler_params=pltpu.CompilerParams(
            collective_id=0, has_side_effects=True, vmem_limit_bytes=60 * 1024 * 1024
        ),
    )(bands.reshape(L, rows, nx), potential.reshape(rows, nx))
    return f.reshape(L, nz, ny, nx), c, p


def solution(mesh):
    in_specs = (P("band", "slab", None, None), P("slab", None, None))
    out_specs = (P("band", "slab", None, None), P("band", None), P("band", None))
    return jax.shard_map(body, mesh=mesh, in_specs=in_specs, out_specs=out_specs, check_vma=False)
```

```python
import functools

import jax
import jax.numpy as jnp
from jax import lax
from jax.experimental import pallas as pl
from jax.experimental.pallas import tpu as pltpu
from jax.sharding import PartitionSpec as P

centre = 4.5
half = 3.5
MESH = pl.DeviceIdType.MESH
STEPS = 4
BELOW, ABOVE = 4, 6


def shifted(v, axis):
    n = v.shape[axis]
    near = pltpu.roll(v, 1, axis) + pltpu.roll(v, n - 1, axis)
    far = pltpu.roll(v, 2, axis) + pltpu.roll(v, n - 2, axis)
    return near, far


def kernel(
    dims, bands, pot, f_out, c_out, p_out,
    e, vbuf, vt, turned, tails, blocks, ends, left, part, rb, rs,
    halo_send, halo_recv, load_sem, out_sem,
    block_send, block_recv, end_send, end_recv,
    row_send, row_recv, slab_send, slab_recv,
):
    nb, ns, L, nz, ny, nx, chunk, active, count, volume = dims
    J = count // 128
    b, s = lax.axis_index("band"), lax.axis_index("slab")
    up, down = lax.rem(s + 1, ns), lax.rem(s + ns - 1, ns)
    inner = pl.ds(BELOW * ny, nz * ny)
    base = BELOW * ny

    load = pltpu.make_async_copy(bands, e.at[0, :, inner], load_sem.at[0])
    load.start()
    load_pot = pltpu.make_async_copy(pot, vbuf.at[inner], load_sem.at[1])
    load_pot.start()

    barrier = pltpu.get_barrier_semaphore()

    def greet_band(d, carry):
        pl.semaphore_signal(
            barrier, inc=1, device_id={"band": lax.rem(b + d, nb)}, device_id_type=MESH
        )
        return carry

    lax.fori_loop(1, nb, greet_band, 0)
    for d in range(1, ns):
        pl.semaphore_signal(
            barrier, inc=1, device_id={"slab": lax.rem(s + d, ns)}, device_id_type=MESH
        )
    pl.semaphore_wait(barrier, nb - 1 + ns - 1)

    stale = base + (nz + 2) * ny
    if base + count > stale:
        spare = base + count - stale
        e[STEPS, :, stale:base + count, :] = jnp.zeros((L, spare, nx), jnp.float32)

    def pushed(src, dst, order, device):
        return pltpu.make_async_remote_copy(
            src_ref=src,
            dst_ref=dst,
            send_sem=halo_send.at[order],
            recv_sem=halo_recv.at[order],
            device_id={"slab": device},
            device_id_type=MESH,
        )

    def span(start, size):
        return pl.ds(start * ny, size * ny)

    def halo(stage, l):
        if stage == 0:
            low, high = bands.at[l, span(0, ABOVE)], bands.at[l, span(nz - BELOW, BELOW)]
        else:
            low, high = e.at[2, l, span(BELOW, ABOVE)], e.at[2, l, span(nz, BELOW)]
        k, order = 2 * stage, 2 * (stage * L + l)
        return (
            pushed(low, e.at[k, l, span(BELOW + nz, ABOVE)], order, down),
            pushed(high, e.at[k, l, span(0, BELOW)], order + 1, up),
        )

    def potential_halo():
        order = 4 * L
        low, high = pot.at[span(0, ABOVE - 2)], pot.at[span(nz - BELOW + 2, BELOW - 2)]
        return (
            pushed(low, vbuf.at[span(BELOW + nz, ABOVE - 2)], order, down),
            pushed(high, vbuf.at[span(2, BELOW - 2)], order + 1, up),
        )

    def plane(k, l, z):
        def rows(offset):
            start = (z + BELOW + offset) * ny
            return slice(start, start + ny)

        scale = (1.0 if k == 0 else 2.0) / half
        diagonal = (vbuf[rows(0), :] + (3.75 - centre)) * scale
        v = e[k, l, rows(0), :]
        near = e[k, l, rows(-1), :] + e[k, l, rows(1), :]
        far = e[k, l, rows(-2), :] + e[k, l, rows(2), :]
        for axis in (0, 1):
            n1, n2 = shifted(v, axis)
            near = near + n1
            far = far + n2
        value = diagonal * v - (scale * 2.0 / 3.0) * near + (scale / 24.0) * far
        if k > 0:
            value = value - e[k - 1, l, rows(0), :]
        e[k + 1, l, rows(0), :] = value

    def first_half(k, l):
        for z in range(2, nz - 2):
            plane(k, l, z)

    def second_half(k, l, stop):
        for z in (*range(-2, 2), *range(nz - 2, nz + 4)):
            plane(k, l, z)
        for z in range(stop):
            plane(k + 1, l, z)

    def send(src, dst, sent, arrived, peer):
        return pltpu.make_async_remote_copy(
            src_ref=src,
            dst_ref=dst,
            send_sem=sent,
            recv_sem=arrived,
            device_id={"band": peer},
            device_id_type=MESH,
        )

    def cells_of(peer):
        return pl.ds(pl.multiple_of(peer * chunk, 8), chunk)

    def block(l):
        return lambda d, peer: send(
            turned.at[:, l, cells_of(peer)], blocks.at[:, b, l],
            block_send.at[l, d], block_recv.at[l, d], peer,
        )

    def end(d, peer):
        return send(tails.at[peer], ends.at[:, b], end_send.at[d], end_recv.at[d], peer)

    def when_active(peer, action):
        if active == nb:
            action()
        else:
            pl.when(peer < active)(action)

    def each_peer(copies, action, everywhere=False):
        def step(d, carry):
            peer = lax.rem(b + d, nb)
            for copy in copies:
                if everywhere:
                    action(copy(d, peer))
                else:
                    when_active(peer, lambda copy=copy: action(copy(d, peer)))
            return carry

        lax.fori_loop(1, nb, step, 0)

    groups = [block(l) for l in range(L)] + [end]

    def turn(j, l):
        turned[j, l] = e[STEPS, l, base + 128 * j:base + 128 * (j + 1), :].T

    def correlate():
        own = cells_of(b)
        for j in range(J):
            blocks[j, b] = turned[j, :, own, :]
        ends[:, b] = tails[b]
        each_peer(groups, lambda copy: copy.wait_recv(), everywhere=True)
        flat = blocks.reshape(J * nb * L * chunk, 128)
        flat_ends = ends.reshape(J * nb * 2 * L, 128)

        def line(r):
            if r < chunk:
                pieces = [
                    flat[pl.ds(j * nb * L * chunk + r, nb * L, stride=chunk), :] for j in range(J)
                ]
            else:
                pieces = [
                    flat_ends[pl.ds(j * nb * 2 * L + r - chunk, nb * L, stride=2), :]
                    for j in range(J)
                ]
            return jnp.concatenate(pieces, axis=1)

        lane = lax.broadcasted_iota(jnp.int32, (nb * L, count), 1)
        y = lane
        for z in range(1, nz + 2):
            y = y - jnp.where(lane >= z * ny, ny, 0)
        inside_slab = lane < nz * ny
        mine = jnp.concatenate([vt[j, own, :] for j in range(J)], axis=1)

        def ahead(x, n):
            return pltpu.roll(x, count - n, 1)

        def split(x):
            high = x.astype(jnp.bfloat16)
            return high, (x - high.astype(jnp.float32)).astype(jnp.bfloat16)

        N = nb * L
        lines = [line(0), line(1)]
        for r in range(chunk):
            lines.append(line(r + 2))
            x = lines[r]
            near = lines[r + 1] + ahead(x, ny)
            near = near + jnp.where(y < ny - 1, ahead(x, 1), pltpu.roll(x, ny - 1, 1))
            far = lines[r + 2] + ahead(x, 2 * ny)
            far = far + jnp.where(y < ny - 2, ahead(x, 2), pltpu.roll(x, ny - 2, 1))
            w = (0.5 * mine[r:r + 1, :] + 1.875) * x - (2.0 / 3.0) * near + (1.0 / 24.0) * far
            x = jnp.where(inside_slab, x, 0.0)
            w = jnp.where(inside_slab, w, 0.0)
            place = pl.ds(r * count, count)
            xh, xl = split(x)
            wh, wl = split(w)
            for i, piece in enumerate((xh, xl, wh, wl)):
                left[i * N:(i + 1) * N, place] = piece
        out = sum(
            lax.dot_general(
                left[...], left[i * N:(i + 1) * N, :], (((1,), (1,)), ((), ())),
                preferred_element_type=jnp.float32,
            )
            for i in (1, 0)
        ) * volume
        gram = out[N:2 * N] + out[:N]
        skew = out[3 * N:] + out[2 * N:3 * N]
        proj = skew + skew.T
        for g in range(nb):
            part[g, 0:L, :] = gram[g * L:(g + 1) * L]
            part[g, L:2 * L, :] = proj[g * L:(g + 1) * L]

    def start(stage, l):
        for copy in halo(stage, l):
            copy.start()

    def arrive(stage, l):
        for copy in halo(stage, l):
            copy.wait_recv()

    def finish_band(l):
        first_half(2, l)
        arrive(1, l)
        second_half(2, l, nz + 2)
        for j in range(J):
            turn(j, l)
        each_peer([block(l)], lambda copy: copy.start())

    for copy in potential_halo():
        copy.start()
    for l in range(min(2, L)):
        start(0, l)
    load.wait()
    load_pot.wait()
    for l in range(L):
        first_half(0, l)
    for copy in potential_halo():
        copy.wait_recv()
    for l in range(L):
        arrive(0, l)
        second_half(0, l, nz)
        start(1, l)
        if l + 2 < L:
            start(0, l + 2)
        if l >= 1:
            finish_band(l - 1)
    finish_band(L - 1)
    for j in range(J):
        vt[j] = vbuf[base + 128 * j:base + 128 * (j + 1), :].T
    result = pltpu.make_async_copy(e.at[STEPS, :, inner], f_out, out_sem)
    result.start()
    for g in range(active):
        after = (g + 1) * chunk % nx
        for j in range(J):
            for l in range(L):
                tails[g, j, 2 * l:2 * l + 2, :] = turned[j, l, after:after + 2, :]
    each_peer([end], lambda copy: copy.start())
    if active == nb:
        correlate()
    else:
        pl.when(b < active)(correlate)

        @pl.when(b >= active)
        def _():
            part[...] = jnp.zeros_like(part)

    def row(d):
        peer = lax.rem(b + d, nb)
        return pltpu.make_async_remote_copy(
            src_ref=part.at[peer],
            dst_ref=rb.at[b],
            send_sem=row_send.at[d],
            recv_sem=row_recv.at[d],
            device_id={"band": peer},
            device_id_type=MESH,
        )

    def each_row(action):
        def step(d, carry):
            action(row(d))
            return carry

        lax.fori_loop(1, nb, step, 0)

    each_row(lambda copy: copy.start())
    rb[b] = part[b]
    each_row(lambda copy: copy.wait_recv())
    rs[s] = jnp.sum(rb[...], axis=0)

    def across(d):
        return pltpu.make_async_remote_copy(
            src_ref=rs.at[s],
            dst_ref=rs.at[s],
            send_sem=slab_send.at[d],
            recv_sem=slab_recv.at[d],
            device_id={"slab": lax.rem(s + d, ns)},
            device_id_type=MESH,
        )

    for d in range(1, ns):
        across(d).start()
    for d in range(1, ns):
        across(d).wait_recv()
    total = rs[0]
    for other in range(1, ns):
        total = total + rs[other]
    c_out[...] = total[:L]
    p_out[...] = total[L:]
    for d in range(1, ns):
        across(d).wait_send()
    each_row(lambda copy: copy.wait_send())
    for copy in potential_halo():
        copy.wait_send()
    for stage in (0, 1):
        for l in range(L):
            for copy in halo(stage, l):
                copy.wait_send()
    each_peer(groups, lambda copy: copy.wait_send())
    result.wait()


def body(bands, potential):
    L, nz, ny, nx = bands.shape
    nb, ns = lax.axis_size("band"), lax.axis_size("slab")
    rows = nz * ny
    tiles = nx // 8
    each = -(-tiles // nb)
    while tiles % each:
        each += 1
    chunk = each * 8
    active = nx // chunk
    count = -(-(nz + 2) * ny // 128) * 128
    J = count // 128
    held = max((nz + BELOW + ABOVE) * ny, BELOW * ny + count)
    dims = (nb, ns, L, nz, ny, nx, chunk, active, count, 1.0 / (rows * ns * nx))
    f32 = jnp.float32
    anywhere, vmem = pl.BlockSpec(memory_space=pl.ANY), pl.BlockSpec(memory_space=pltpu.VMEM)
    dma = pltpu.SemaphoreType.DMA
    f, c, p = pl.pallas_call(
        functools.partial(kernel, dims),
        out_shape=(
            pltpu.VMEM((L, rows, nx), f32),
            pltpu.VMEM((L, nb * L), f32),
            pltpu.VMEM((L, nb * L), f32),
        ),
        in_specs=[pl.BlockSpec(memory_space=pltpu.HBM)] * 2,
        out_specs=(anywhere, vmem, vmem),
        scratch_shapes=[
            pltpu.VMEM((STEPS + 1, L, held, nx), f32),
            pltpu.VMEM((held, nx), f32),
            pltpu.VMEM((J, nx, 128), f32),
            pltpu.VMEM((J, L, nx, 128), f32),
            pltpu.VMEM((nb, J, 2 * L, 128), f32),
            pltpu.VMEM((J, nb, L, chunk, 128), f32),
            pltpu.VMEM((J, nb, 2 * L, 128), f32),
            pltpu.VMEM((4 * nb * L, chunk * count), jnp.bfloat16),
            pltpu.VMEM((nb, 2 * L, nb * L), f32),
            pltpu.VMEM((nb, 2 * L, nb * L), f32),
            pltpu.VMEM((ns, 2 * L, nb * L), f32),
            dma((4 * L + 2,)), dma((4 * L + 2,)),
            dma((2,)), dma,
            dma((L, nb)), dma((L, nb)),
            dma((nb,)), dma((nb,)),
            dma((nb,)), dma((nb,)),
            dma((ns,)), dma((ns,)),
        ],
        compiler_params=pltpu.CompilerParams(
            collective_id=0, has_side_effects=True, vmem_limit_bytes=60 * 1024 * 1024
        ),
    )(bands.reshape(L, rows, nx), potential.reshape(rows, nx))
    return f.reshape(L, nz, ny, nx), c, p


def solution(mesh):
    in_specs = (P("band", "slab", None, None), P("slab", None, None))
    out_specs = (P("band", "slab", None, None), P("band", None), P("band", None))
    return jax.shard_map(body, mesh=mesh, in_specs=in_specs, out_specs=out_specs, check_vma=False)
```

```python
import functools

import jax
import jax.numpy as jnp
from jax import lax
from jax.experimental import pallas as pl
from jax.experimental.pallas import tpu as pltpu
from jax.sharding import PartitionSpec as P

centre = 4.5
half = 3.5
MESH = pl.DeviceIdType.MESH
STEPS = 4
BELOW, ABOVE = 4, 6


def shifted(v, axis):
    n = v.shape[axis]
    near = pltpu.roll(v, 1, axis) + pltpu.roll(v, n - 1, axis)
    far = pltpu.roll(v, 2, axis) + pltpu.roll(v, n - 2, axis)
    return near, far


def kernel(
    dims, bands, pot, f_out, c_out, p_out,
    e, vbuf, vt, turned, tails, blocks, ends, left, part, rb, rs,
    halo_send, halo_recv, load_sem, out_sem,
    block_send, block_recv, end_send, end_recv,
    row_send, row_recv, slab_send, slab_recv,
):
    nb, ns, L, nz, ny, nx, chunk, active, count, volume = dims
    J = count // 128
    b, s = lax.axis_index("band"), lax.axis_index("slab")
    up, down = lax.rem(s + 1, ns), lax.rem(s + ns - 1, ns)
    inner = pl.ds(BELOW * ny, nz * ny)
    base = BELOW * ny

    load = pltpu.make_async_copy(bands, e.at[0, :, inner], load_sem.at[0])
    load.start()
    load_pot = pltpu.make_async_copy(pot, vbuf.at[inner], load_sem.at[1])
    load_pot.start()

    barrier = pltpu.get_barrier_semaphore()

    def greet_band(d, carry):
        pl.semaphore_signal(
            barrier, inc=1, device_id={"band": lax.rem(b + d, nb)}, device_id_type=MESH
        )
        return carry

    lax.fori_loop(1, nb, greet_band, 0)
    for d in range(1, ns):
        pl.semaphore_signal(
            barrier, inc=1, device_id={"slab": lax.rem(s + d, ns)}, device_id_type=MESH
        )
    pl.semaphore_wait(barrier, nb - 1 + ns - 1)

    stale = base + (nz + 2) * ny
    if base + count > stale:
        spare = base + count - stale
        e[STEPS, :, stale:base + count, :] = jnp.zeros((L, spare, nx), jnp.float32)

    def pushed(src, dst, order, device):
        return pltpu.make_async_remote_copy(
            src_ref=src,
            dst_ref=dst,
            send_sem=halo_send.at[order],
            recv_sem=halo_recv.at[order],
            device_id={"slab": device},
            device_id_type=MESH,
        )

    def span(start, size):
        return pl.ds(start * ny, size * ny)

    def halo(stage, l):
        if stage == 0:
            low, high = bands.at[l, span(0, ABOVE)], bands.at[l, span(nz - BELOW, BELOW)]
        else:
            low, high = e.at[2, l, span(BELOW, ABOVE)], e.at[2, l, span(nz, BELOW)]
        k, order = 2 * stage, 2 * (stage * L + l)
        return (
            pushed(low, e.at[k, l, span(BELOW + nz, ABOVE)], order, down),
            pushed(high, e.at[k, l, span(0, BELOW)], order + 1, up),
        )

    def potential_halo():
        order = 4 * L
        low, high = pot.at[span(0, ABOVE - 2)], pot.at[span(nz - BELOW + 2, BELOW - 2)]
        return (
            pushed(low, vbuf.at[span(BELOW + nz, ABOVE - 2)], order, down),
            pushed(high, vbuf.at[span(2, BELOW - 2)], order + 1, up),
        )

    def plane(k, l, z):
        def rows(offset):
            start = (z + BELOW + offset) * ny
            return slice(start, start + ny)

        scale = (1.0 if k == 0 else 2.0) / half
        diagonal = (vbuf[rows(0), :] + (3.75 - centre)) * scale
        v = e[k, l, rows(0), :]
        near = e[k, l, rows(-1), :] + e[k, l, rows(1), :]
        far = e[k, l, rows(-2), :] + e[k, l, rows(2), :]
        for axis in (0, 1):
            n1, n2 = shifted(v, axis)
            near = near + n1
            far = far + n2
        value = diagonal * v - (scale * 2.0 / 3.0) * near + (scale / 24.0) * far
        if k > 0:
            value = value - e[k - 1, l, rows(0), :]
        e[k + 1, l, rows(0), :] = value

    def first_half(k, l):
        for z in range(2, nz - 2):
            plane(k, l, z)

    def second_half(k, l, stop):
        for z in (*range(-2, 2), *range(nz - 2, nz + 4)):
            plane(k, l, z)
        for z in range(stop):
            plane(k + 1, l, z)

    def send(src, dst, sent, arrived, peer):
        return pltpu.make_async_remote_copy(
            src_ref=src,
            dst_ref=dst,
            send_sem=sent,
            recv_sem=arrived,
            device_id={"band": peer},
            device_id_type=MESH,
        )

    def cells_of(peer):
        return pl.ds(pl.multiple_of(peer * chunk, 8), chunk)

    def block(l):
        return lambda d, peer: send(
            turned.at[:, l, cells_of(peer)], blocks.at[:, b, l],
            block_send.at[l, d], block_recv.at[l, d], peer,
        )

    def end(d, peer):
        return send(tails.at[peer], ends.at[:, b], end_send.at[d], end_recv.at[d], peer)

    def when_active(peer, action):
        if active == nb:
            action()
        else:
            pl.when(peer < active)(action)

    def partner(d):
        if nb & (nb - 1):
            return lax.rem(b + d, nb)
        peer, bit = 0, 1
        while bit < nb:
            peer = peer + lax.rem(lax.div(b, bit) + lax.div(nb - d, bit), 2) * bit
            bit *= 2
        return peer

    def each_peer(copies, action, everywhere=False):
        def step(d, carry):
            peer = partner(d)
            for copy in copies:
                if everywhere:
                    action(copy(d, peer))
                else:
                    when_active(peer, lambda copy=copy: action(copy(d, peer)))
            return carry

        lax.fori_loop(1, nb, step, 0)

    groups = [block(l) for l in range(L)] + [end]

    def turn(j, l):
        turned[j, l] = e[STEPS, l, base + 128 * j:base + 128 * (j + 1), :].T

    def correlate():
        own = cells_of(b)
        for j in range(J):
            blocks[j, b] = turned[j, :, own, :]
        ends[:, b] = tails[b]
        each_peer(groups, lambda copy: copy.wait_recv(), everywhere=True)
        flat = blocks.reshape(J * nb * L * chunk, 128)
        flat_ends = ends.reshape(J * nb * 2 * L, 128)

        def line(r):
            if r < chunk:
                pieces = [
                    flat[pl.ds(j * nb * L * chunk + r, nb * L, stride=chunk), :] for j in range(J)
                ]
            else:
                pieces = [
                    flat_ends[pl.ds(j * nb * 2 * L + r - chunk, nb * L, stride=2), :]
                    for j in range(J)
                ]
            return jnp.concatenate(pieces, axis=1)

        lane = lax.broadcasted_iota(jnp.int32, (nb * L, count), 1)
        y = lane
        for z in range(1, nz + 2):
            y = y - jnp.where(lane >= z * ny, ny, 0)
        inside_slab = lane < nz * ny
        mine = jnp.concatenate([vt[j, own, :] for j in range(J)], axis=1)

        def ahead(x, n):
            return pltpu.roll(x, count - n, 1)

        def split(x):
            high = x.astype(jnp.bfloat16)
            return high, (x - high.astype(jnp.float32)).astype(jnp.bfloat16)

        N = nb * L
        lines = [line(0), line(1)]
        for r in range(chunk):
            lines.append(line(r + 2))
            x = lines[r]
            near = lines[r + 1] + ahead(x, ny)
            near = near + jnp.where(y < ny - 1, ahead(x, 1), pltpu.roll(x, ny - 1, 1))
            far = lines[r + 2] + ahead(x, 2 * ny)
            far = far + jnp.where(y < ny - 2, ahead(x, 2), pltpu.roll(x, ny - 2, 1))
            w = (0.5 * mine[r:r + 1, :] + 1.875) * x - (2.0 / 3.0) * near + (1.0 / 24.0) * far
            x = jnp.where(inside_slab, x, 0.0)
            w = jnp.where(inside_slab, w, 0.0)
            place = pl.ds(r * count, count)
            xh, xl = split(x)
            wh, wl = split(w)
            for i, piece in enumerate((xh, xl, wh, wl)):
                left[i * N:(i + 1) * N, place] = piece
        out = lax.dot_general(
            left[...], left[0:2 * N, :], (((1,), (1,)), ((), ())),
            preferred_element_type=jnp.float32,
        )
        out = (out[:, N:] + out[:, :N]) * volume
        gram = out[N:2 * N] + out[:N]
        skew = out[3 * N:] + out[2 * N:3 * N]
        proj = skew + skew.T
        for g in range(nb):
            part[g, 0:L, :] = gram[g * L:(g + 1) * L]
            part[g, L:2 * L, :] = proj[g * L:(g + 1) * L]

    def start(stage, l):
        for copy in halo(stage, l):
            copy.start()

    def arrive(stage, l):
        for copy in halo(stage, l):
            copy.wait_recv()

    def finish_band(l):
        first_half(2, l)
        arrive(1, l)
        second_half(2, l, nz + 2)
        for j in range(J):
            turn(j, l)
        each_peer([block(l)], lambda copy: copy.start())

    for copy in potential_halo():
        copy.start()
    for l in range(min(2, L)):
        start(0, l)
    load.wait()
    load_pot.wait()
    for l in range(L):
        first_half(0, l)
    for copy in potential_halo():
        copy.wait_recv()
    for l in range(L):
        arrive(0, l)
        second_half(0, l, nz)
        start(1, l)
        if l + 2 < L:
            start(0, l + 2)
        if l >= 1:
            finish_band(l - 1)
    finish_band(L - 1)
    for j in range(J):
        vt[j] = vbuf[base + 128 * j:base + 128 * (j + 1), :].T
    result = pltpu.make_async_copy(e.at[STEPS, :, inner], f_out, out_sem)
    result.start()
    for g in range(active):
        after = (g + 1) * chunk % nx
        for j in range(J):
            for l in range(L):
                tails[g, j, 2 * l:2 * l + 2, :] = turned[j, l, after:after + 2, :]
    each_peer([end], lambda copy: copy.start())
    if active == nb:
        correlate()
    else:
        pl.when(b < active)(correlate)

        @pl.when(b >= active)
        def _():
            part[...] = jnp.zeros_like(part)

    def row(d):
        peer = lax.rem(b + d, nb)
        return pltpu.make_async_remote_copy(
            src_ref=part.at[peer],
            dst_ref=rb.at[b],
            send_sem=row_send.at[d],
            recv_sem=row_recv.at[d],
            device_id={"band": peer},
            device_id_type=MESH,
        )

    def each_row(action):
        def step(d, carry):
            action(row(d))
            return carry

        lax.fori_loop(1, nb, step, 0)

    each_row(lambda copy: copy.start())
    rb[b] = part[b]
    each_row(lambda copy: copy.wait_recv())
    rs[s] = jnp.sum(rb[...], axis=0)

    def across(d):
        return pltpu.make_async_remote_copy(
            src_ref=rs.at[s],
            dst_ref=rs.at[s],
            send_sem=slab_send.at[d],
            recv_sem=slab_recv.at[d],
            device_id={"slab": lax.rem(s + d, ns)},
            device_id_type=MESH,
        )

    for d in range(1, ns):
        across(d).start()
    for d in range(1, ns):
        across(d).wait_recv()
    total = rs[0]
    for other in range(1, ns):
        total = total + rs[other]
    c_out[...] = total[:L]
    p_out[...] = total[L:]
    for d in range(1, ns):
        across(d).wait_send()
    each_row(lambda copy: copy.wait_send())
    for copy in potential_halo():
        copy.wait_send()
    for stage in (0, 1):
        for l in range(L):
            for copy in halo(stage, l):
                copy.wait_send()
    each_peer(groups, lambda copy: copy.wait_send())
    result.wait()


def body(bands, potential):
    L, nz, ny, nx = bands.shape
    nb, ns = lax.axis_size("band"), lax.axis_size("slab")
    rows = nz * ny
    tiles = nx // 8
    each = -(-tiles // nb)
    while tiles % each:
        each += 1
    chunk = each * 8
    active = nx // chunk
    count = -(-(nz + 2) * ny // 128) * 128
    J = count // 128
    held = max((nz + BELOW + ABOVE) * ny, BELOW * ny + count)
    dims = (nb, ns, L, nz, ny, nx, chunk, active, count, 1.0 / (rows * ns * nx))
    f32 = jnp.float32
    anywhere, vmem = pl.BlockSpec(memory_space=pl.ANY), pl.BlockSpec(memory_space=pltpu.VMEM)
    dma = pltpu.SemaphoreType.DMA
    f, c, p = pl.pallas_call(
        functools.partial(kernel, dims),
        out_shape=(
            pltpu.VMEM((L, rows, nx), f32),
            pltpu.VMEM((L, nb * L), f32),
            pltpu.VMEM((L, nb * L), f32),
        ),
        in_specs=[pl.BlockSpec(memory_space=pltpu.HBM)] * 2,
        out_specs=(anywhere, vmem, vmem),
        scratch_shapes=[
            pltpu.VMEM((STEPS + 1, L, held, nx), f32),
            pltpu.VMEM((held, nx), f32),
            pltpu.VMEM((J, nx, 128), f32),
            pltpu.VMEM((J, L, nx, 128), f32),
            pltpu.VMEM((nb, J, 2 * L, 128), f32),
            pltpu.VMEM((J, nb, L, chunk, 128), f32),
            pltpu.VMEM((J, nb, 2 * L, 128), f32),
            pltpu.VMEM((4 * nb * L, chunk * count), jnp.bfloat16),
            pltpu.VMEM((nb, 2 * L, nb * L), f32),
            pltpu.VMEM((nb, 2 * L, nb * L), f32),
            pltpu.VMEM((ns, 2 * L, nb * L), f32),
            dma((4 * L + 2,)), dma((4 * L + 2,)),
            dma((2,)), dma,
            dma((L, nb)), dma((L, nb)),
            dma((nb,)), dma((nb,)),
            dma((nb,)), dma((nb,)),
            dma((ns,)), dma((ns,)),
        ],
        compiler_params=pltpu.CompilerParams(
            collective_id=0, has_side_effects=True, vmem_limit_bytes=60 * 1024 * 1024
        ),
    )(bands.reshape(L, rows, nx), potential.reshape(rows, nx))
    return f.reshape(L, nz, ny, nx), c, p


def solution(mesh):
    in_specs = (P("band", "slab", None, None), P("slab", None, None))
    out_specs = (P("band", "slab", None, None), P("band", None), P("band", None))
    return jax.shard_map(body, mesh=mesh, in_specs=in_specs, out_specs=out_specs, check_vma=False)
```

```python
import functools

import jax
import jax.numpy as jnp
from jax import lax
from jax.experimental import pallas as pl
from jax.experimental.pallas import tpu as pltpu
from jax.sharding import PartitionSpec as P

centre = 4.5
half = 3.5
MESH = pl.DeviceIdType.MESH
STEPS = 4
BELOW, ABOVE = 4, 6


def shifted(v, axis):
    n = v.shape[axis]
    near = pltpu.roll(v, 1, axis) + pltpu.roll(v, n - 1, axis)
    far = pltpu.roll(v, 2, axis) + pltpu.roll(v, n - 2, axis)
    return near, far


def kernel(
    dims, bands, pot, f_out, c_out, p_out,
    e, vbuf, vt, turned, tails, blocks, ends, left, part, rb,
    halo_send, halo_recv, load_sem, out_sem,
    block_send, block_recv, end_send, end_recv,
    row_send, row_recv,
):
    nb, ns, L, nz, ny, nx, chunk, active, count, volume = dims
    J = count // 128
    b, s = lax.axis_index("band"), lax.axis_index("slab")
    up, down = lax.rem(s + 1, ns), lax.rem(s + ns - 1, ns)
    inner = pl.ds(BELOW * ny, nz * ny)
    base = BELOW * ny

    load = pltpu.make_async_copy(bands, e.at[0, :, inner], load_sem.at[0])
    load.start()
    load_pot = pltpu.make_async_copy(pot, vbuf.at[inner], load_sem.at[1])
    load_pot.start()

    barrier = pltpu.get_barrier_semaphore()

    for t in range(ns):
        def greet(d, carry, t=t):
            pl.semaphore_signal(
                barrier, inc=1,
                device_id={"band": lax.rem(b + d, nb), "slab": lax.rem(s + t, ns)},
                device_id_type=MESH,
            )
            return carry

        lax.fori_loop(0 if t else 1, nb, greet, 0)
    pl.semaphore_wait(barrier, nb * ns - 1)
    stale = base + (nz + 2) * ny
    if base + count > stale:
        spare = base + count - stale
        e[STEPS, :, stale:base + count, :] = jnp.zeros((L, spare, nx), jnp.float32)

    def pushed(src, dst, order, device):
        return pltpu.make_async_remote_copy(
            src_ref=src,
            dst_ref=dst,
            send_sem=halo_send.at[order],
            recv_sem=halo_recv.at[order],
            device_id={"slab": device},
            device_id_type=MESH,
        )

    def span(start, size):
        return pl.ds(start * ny, size * ny)

    def halo(stage, l):
        if stage == 0:
            low, high = bands.at[l, span(0, ABOVE)], bands.at[l, span(nz - BELOW, BELOW)]
        else:
            low, high = e.at[2, l, span(BELOW, ABOVE)], e.at[2, l, span(nz, BELOW)]
        k, order = 2 * stage, 2 * (stage * L + l)
        return (
            pushed(low, e.at[k, l, span(BELOW + nz, ABOVE)], order, down),
            pushed(high, e.at[k, l, span(0, BELOW)], order + 1, up),
        )

    def potential_halo():
        order = 4 * L
        low, high = pot.at[span(0, ABOVE - 2)], pot.at[span(nz - BELOW + 2, BELOW - 2)]
        return (
            pushed(low, vbuf.at[span(BELOW + nz, ABOVE - 2)], order, down),
            pushed(high, vbuf.at[span(2, BELOW - 2)], order + 1, up),
        )

    def plane(k, l, z):
        def rows(offset):
            start = (z + BELOW + offset) * ny
            return slice(start, start + ny)

        scale = (1.0 if k == 0 else 2.0) / half
        diagonal = (vbuf[rows(0), :] + (3.75 - centre)) * scale
        v = e[k, l, rows(0), :]
        near = e[k, l, rows(-1), :] + e[k, l, rows(1), :]
        far = e[k, l, rows(-2), :] + e[k, l, rows(2), :]
        for axis in (0, 1):
            n1, n2 = shifted(v, axis)
            near = near + n1
            far = far + n2
        value = diagonal * v - (scale * 2.0 / 3.0) * near + (scale / 24.0) * far
        if k > 0:
            value = value - e[k - 1, l, rows(0), :]
        e[k + 1, l, rows(0), :] = value

    def first_half(k, l):
        for z in range(2, nz - 2):
            plane(k, l, z)

    def second_half(k, l, stop):
        for z in (*range(-2, 2), *range(nz - 2, nz + 4)):
            plane(k, l, z)
        for z in range(stop):
            plane(k + 1, l, z)

    def send(src, dst, sent, arrived, peer):
        return pltpu.make_async_remote_copy(
            src_ref=src,
            dst_ref=dst,
            send_sem=sent,
            recv_sem=arrived,
            device_id={"band": peer},
            device_id_type=MESH,
        )

    def cells_of(peer):
        return pl.ds(pl.multiple_of(peer * chunk, 8), chunk)

    def block(l):
        return lambda d, peer: send(
            turned.at[:, l, cells_of(peer)], blocks.at[:, b, l],
            block_send.at[l, d], block_recv.at[l, d], peer,
        )

    def end(d, peer):
        return send(tails.at[peer], ends.at[:, b], end_send.at[d], end_recv.at[d], peer)

    def when_active(peer, action):
        if active == nb:
            action()
        else:
            pl.when(peer < active)(action)

    def partner(d):
        if nb & (nb - 1):
            return lax.rem(b + d, nb)
        peer, bit = 0, 1
        while bit < nb:
            peer = peer + lax.rem(lax.div(b, bit) + lax.div(nb - d, bit), 2) * bit
            bit *= 2
        return peer

    def each_peer(copies, action, everywhere=False):
        def step(d, carry):
            peer = partner(d)
            for copy in copies:
                if everywhere:
                    action(copy(d, peer))
                else:
                    when_active(peer, lambda copy=copy: action(copy(d, peer)))
            return carry

        lax.fori_loop(1, nb, step, 0)

    groups = [block(l) for l in range(L)] + [end]

    def turn(j, l):
        turned[j, l] = e[STEPS, l, base + 128 * j:base + 128 * (j + 1), :].T

    def correlate():
        own = cells_of(b)
        for j in range(J):
            blocks[j, b] = turned[j, :, own, :]
        ends[:, b] = tails[b]
        each_peer(groups, lambda copy: copy.wait_recv(), everywhere=True)
        flat = blocks.reshape(J * nb * L * chunk, 128)
        flat_ends = ends.reshape(J * nb * 2 * L, 128)

        def line(r):
            if r < chunk:
                pieces = [
                    flat[pl.ds(j * nb * L * chunk + r, nb * L, stride=chunk), :] for j in range(J)
                ]
            else:
                pieces = [
                    flat_ends[pl.ds(j * nb * 2 * L + r - chunk, nb * L, stride=2), :]
                    for j in range(J)
                ]
            return jnp.concatenate(pieces, axis=1)

        lane = lax.broadcasted_iota(jnp.int32, (nb * L, count), 1)
        y = lane
        for z in range(1, nz + 2):
            y = y - jnp.where(lane >= z * ny, ny, 0)
        inside_slab = lane < nz * ny
        mine = jnp.concatenate([vt[j, own, :] for j in range(J)], axis=1)

        def ahead(x, n):
            return pltpu.roll(x, count - n, 1)

        def split(x):
            high = x.astype(jnp.bfloat16)
            return high, (x - high.astype(jnp.float32)).astype(jnp.bfloat16)

        N = nb * L
        lines = [line(0), line(1)]
        for r in range(chunk):
            lines.append(line(r + 2))
            x = lines[r]
            near = lines[r + 1] + ahead(x, ny)
            near = near + jnp.where(y < ny - 1, ahead(x, 1), pltpu.roll(x, ny - 1, 1))
            far = lines[r + 2] + ahead(x, 2 * ny)
            far = far + jnp.where(y < ny - 2, ahead(x, 2), pltpu.roll(x, ny - 2, 1))
            w = (0.5 * mine[r:r + 1, :] + 1.875) * x - (2.0 / 3.0) * near + (1.0 / 24.0) * far
            x = jnp.where(inside_slab, x, 0.0)
            w = jnp.where(inside_slab, w, 0.0)
            place = pl.ds(r * count, count)
            xh, xl = split(x)
            wh, wl = split(w)
            for i, piece in enumerate((xh, xl, wh, wl)):
                left[i * N:(i + 1) * N, place] = piece
        out = lax.dot_general(
            left[...], left[0:2 * N, :], (((1,), (1,)), ((), ())),
            preferred_element_type=jnp.float32,
        )
        out = (out[:, N:] + out[:, :N]) * volume
        gram = out[N:2 * N] + out[:N]
        skew = out[3 * N:] + out[2 * N:3 * N]
        proj = skew + skew.T
        for g in range(nb):
            part[g, 0:L, :] = gram[g * L:(g + 1) * L]
            part[g, L:2 * L, :] = proj[g * L:(g + 1) * L]

    def start(stage, l):
        for copy in halo(stage, l):
            copy.start()

    def arrive(stage, l):
        for copy in halo(stage, l):
            copy.wait_recv()

    def finish_band(l):
        first_half(2, l)
        arrive(1, l)
        second_half(2, l, nz + 2)
        for j in range(J):
            turn(j, l)
        each_peer([block(l)], lambda copy: copy.start())

    for copy in potential_halo():
        copy.start()
    for l in range(min(2, L)):
        start(0, l)
    load.wait()
    load_pot.wait()
    for l in range(L):
        first_half(0, l)
    for copy in potential_halo():
        copy.wait_recv()
    for l in range(L):
        arrive(0, l)
        second_half(0, l, nz)
        start(1, l)
        if l + 2 < L:
            start(0, l + 2)
        if l >= 1:
            finish_band(l - 1)
    finish_band(L - 1)
    for j in range(J):
        vt[j] = vbuf[base + 128 * j:base + 128 * (j + 1), :].T
    result = pltpu.make_async_copy(e.at[STEPS, :, inner], f_out, out_sem)
    result.start()
    for g in range(active):
        after = (g + 1) * chunk % nx
        for j in range(J):
            for l in range(L):
                tails[g, j, 2 * l:2 * l + 2, :] = turned[j, l, after:after + 2, :]
    each_peer([end], lambda copy: copy.start())
    if active == nb:
        correlate()
    else:
        pl.when(b < active)(correlate)

        @pl.when(b >= active)
        def _():
            part[...] = jnp.zeros_like(part)

    def row(t, d):
        peer = lax.rem(b + d, nb)
        return pltpu.make_async_remote_copy(
            src_ref=part.at[peer],
            dst_ref=rb.at[s, b],
            send_sem=row_send.at[t, d],
            recv_sem=row_recv.at[t, d],
            device_id={"band": peer, "slab": lax.rem(s + t, ns)},
            device_id_type=MESH,
        )

    def each_row(action):
        for t in range(ns):
            def step(d, carry, t=t):
                action(row(t, d))
                return carry

            lax.fori_loop(0 if t else 1, nb, step, 0)

    each_row(lambda copy: copy.start())
    rb[s, b] = part[b]
    each_row(lambda copy: copy.wait_recv())
    total = jnp.sum(rb[...], axis=(0, 1))
    c_out[...] = total[:L]
    p_out[...] = total[L:]
    each_row(lambda copy: copy.wait_send())
    for copy in potential_halo():
        copy.wait_send()
    for stage in (0, 1):
        for l in range(L):
            for copy in halo(stage, l):
                copy.wait_send()
    each_peer(groups, lambda copy: copy.wait_send())
    result.wait()


def body(bands, potential):
    L, nz, ny, nx = bands.shape
    nb, ns = lax.axis_size("band"), lax.axis_size("slab")
    rows = nz * ny
    tiles = nx // 8
    each = -(-tiles // nb)
    while tiles % each:
        each += 1
    chunk = each * 8
    active = nx // chunk
    count = -(-(nz + 2) * ny // 128) * 128
    J = count // 128
    held = max((nz + BELOW + ABOVE) * ny, BELOW * ny + count)
    dims = (nb, ns, L, nz, ny, nx, chunk, active, count, 1.0 / (rows * ns * nx))
    f32 = jnp.float32
    anywhere, vmem = pl.BlockSpec(memory_space=pl.ANY), pl.BlockSpec(memory_space=pltpu.VMEM)
    dma = pltpu.SemaphoreType.DMA
    f, c, p = pl.pallas_call(
        functools.partial(kernel, dims),
        out_shape=(
            pltpu.VMEM((L, rows, nx), f32),
            pltpu.VMEM((L, nb * L), f32),
            pltpu.VMEM((L, nb * L), f32),
        ),
        in_specs=[pl.BlockSpec(memory_space=pltpu.HBM)] * 2,
        out_specs=(anywhere, vmem, vmem),
        scratch_shapes=[
            pltpu.VMEM((STEPS + 1, L, held, nx), f32),
            pltpu.VMEM((held, nx), f32),
            pltpu.VMEM((J, nx, 128), f32),
            pltpu.VMEM((J, L, nx, 128), f32),
            pltpu.VMEM((nb, J, 2 * L, 128), f32),
            pltpu.VMEM((J, nb, L, chunk, 128), f32),
            pltpu.VMEM((J, nb, 2 * L, 128), f32),
            pltpu.VMEM((4 * nb * L, chunk * count), jnp.bfloat16),
            pltpu.VMEM((nb, 2 * L, nb * L), f32),
            pltpu.VMEM((ns, nb, 2 * L, nb * L), f32),
            dma((4 * L + 2,)), dma((4 * L + 2,)),
            dma((2,)), dma,
            dma((L, nb)), dma((L, nb)),
            dma((nb,)), dma((nb,)),
            dma((ns, nb)), dma((ns, nb)),
        ],
        compiler_params=pltpu.CompilerParams(
            collective_id=0, has_side_effects=True, vmem_limit_bytes=60 * 1024 * 1024
        ),
    )(bands.reshape(L, rows, nx), potential.reshape(rows, nx))
    return f.reshape(L, nz, ny, nx), c, p


def solution(mesh):
    in_specs = (P("band", "slab", None, None), P("slab", None, None))
    out_specs = (P("band", "slab", None, None), P("band", None), P("band", None))
    return jax.shard_map(body, mesh=mesh, in_specs=in_specs, out_specs=out_specs, check_vma=False)
```
